512 devices in a mesh: dp: 32 (over z, core), expert: 16 (over x, y).
Axes of the slice: x: 4, y: 4, z: 16, core: 2. Of those that a mesh axis runs over, the one named last changes fastest.
Arguments:
- tokens: bfloat16 [65536, 2560], P(('dp', 'expert')), may hold values from -24 to 24
- out_grad: bfloat16 [65536, 2560], P(('dp', 'expert')), may hold values from -0.29882812 to 0.29882812
- gate_up: bfloat16 [65536, 1, 1536], P(('dp', 'expert')), may hold values from -8 to 8
- route_weight: bfloat16 [65536, 1], P(('dp', 'expert')), may hold values from 0.19921875 to 1
- routes: int32 [65536, 1], P(('dp', 'expert')), may hold values from 0 to 15; in each aligned block of 128 rows (0 to 127, 128 to 255, ...) at most 16 rows name the same one
- down_weight: bfloat16 [16, 768, 2560], P('expert', 'dp'), may hold values from -0.21875 to 0.21875
- master: float32 [16, 32, 126720], P('expert', 'dp'), may hold values from -0.12 to 0.12
- moment_one: float32 [16, 32, 126720], P('expert', 'dp'), may hold values from -2 to 2
- moment_two: float32 [16, 32, 126720], P('expert', 'dp'), may hold values from 0.05 to 5
- offsets: int32 [33], replicated, may hold values from 0 to 3932160, as said below
Outputs:
- new_master: float32 [16, 32, 126720], P('expert', 'dp')
- new_moment_one: float32 [16, 32, 126720], P('expert', 'dp')
- new_moment_two: float32 [16, 32, 126720], P('expert', 'dp')
- new_weight: bfloat16 [16, 2560, 1536], P('expert', 'dp')
- router_grad: float32 [65536, 1], P(('dp', 'expert'))
The draws below stay inside these ranges and needn't reach their ends.
Inputs may be any that keep to these rules, and one draw needn't show every extreme that they name: `routes`: in each aligned block of 128 tokens (the tokens of one device) no expert is named more than 16 times, a bound that some block reaches; the 1 choices of a token differ. offsets[0] = 0, offsets[32] = 3932160; for 0 < j < 32, offsets[j] lies from j * 122880 - 3840 to j * 122880 - 2; offsets[31] = 3805440, so the last bucket holds exactly 126720 entries.
All inputs are finite; a program needn't handle non-finite values.
Results may differ from the reference program's by a relative error of at most 0.0012.
Values may be sent and summed in bfloat16 or wider, within the bound.
A program may use at most 128 MiB of HBM per device.

```python
import math
import jax
import jax.numpy as jnp
import numpy as np
from jax import lax

D = 2560
F = 768
TOPK = 1
TOK_DEV = 128
EXPERTS = 16
TOKENS = 65536
CAP = 16
TWO_F = 1536
BUCKETS = 32
SPAN = 122880
SLACK = 3840
BCAP = 126720
N_DP = 32
N_EXPERT = 16


def draw_offsets(key, part):
    key = jax.random.fold_in(key, 7)
    sizes_drawn = jax.random.randint(key, (BUCKETS + 1,), 2, SLACK + 1).astype(jnp.int32)
    places = jnp.arange(BUCKETS + 1, dtype=jnp.int32)
    shifts = jnp.where(places == BUCKETS - 1, SLACK, sizes_drawn).astype(jnp.int32)
    shifts = jnp.where((places == 0) | (places == BUCKETS), 0, shifts).astype(jnp.int32)
    return (places * SPAN - shifts).astype(jnp.int32)


def with_spikes(values, key, source, target, blocks, factor):
    def block_of(dim):
        return (jnp.arange(values.shape[dim]) // (values.shape[dim] // blocks)).reshape((-1,) + (1,) * (values.ndim - 1 - dim))

    near = jax.random.permutation(key, blocks)[block_of(target)]
    far = (block_of(target) + blocks // 2) % blocks
    return jnp.where((block_of(source) == near) | (block_of(source) == far), factor * values, values)


def steps_of(own_key, extent, shards, smallest, high):
    def one(axis_at, parts):
        heights = jax.random.uniform(jax.random.fold_in(jax.random.fold_in(own_key, 6), axis_at), (parts,), jnp.float32, smallest / len(shards), high / len(shards))
        return jnp.repeat(jnp.exp(heights), extent[axis_at] // parts).reshape((-1,) + (1,) * (len(extent) - axis_at - 1))

    loudness = one(*shards[0])
    for cut in shards[1:]:
        loudness = loudness * one(*cut)
    return loudness


def shared_out(stream_key, own, number, rows, number_of, top, most, slope):
    sequence = jax.random.permutation(stream_key, number_of)
    heavy_load, ordinary = shares(number_of, rows * top, most, slope, True), shares(number_of, rows * top, most, slope, False)
    places = jnp.arange(number_of)

    def named(sizes, rotation):
        used = int((sizes > 0).sum())
        fixed = max(1, used // 4)
        passed = fixed + (places - fixed + rotation * (used - fixed)) % max(1, number_of - fixed)
        return jnp.zeros((number_of,), jnp.int32).at[sequence[jnp.where(places < fixed, places, passed)]].set(jnp.asarray(sizes, jnp.int32))

    sizes = jnp.where(number % 4 == 0, named(heavy_load, number // 4), named(ordinary, number - number // 4 - 1))
    mixed = jax.random.permutation(jax.random.fold_in(own, 3), number_of)
    source_of, taker = mixed[0:number_of // 2 * 2:2], mixed[1:number_of // 2 * 2:2]
    room = jnp.minimum(sizes[source_of] - 1, most - sizes[taker]) // 2
    room = jnp.where((source_of == sequence[0]) | (taker == sequence[0]) | (sizes[taker] == 0), 0, jnp.maximum(room, 0))
    passed = jax.random.randint(jax.random.fold_in(own, 4), (number_of // 2,), 0, 1 << 20) % (room + 1)
    sizes = sizes.at[source_of].add(-passed).at[taker].add(passed)
    items = jnp.searchsorted(jnp.cumsum(sizes), jnp.arange(rows * top), side="right").astype(jnp.int32)
    listing = items.reshape(top, rows).T
    listing = listing[jax.random.permutation(jax.random.fold_in(own, 1), rows)]
    rotation = jax.random.randint(jax.random.fold_in(own, 2), (rows, 1), 0, top)
    return jnp.take_along_axis(listing, (jnp.arange(top)[None, :] + rotation) % top, axis=1)


def shares(count, total, reach, lean, full):
    weights = [(1 << 20) // math.isqrt(rank ** lean) + 1 for rank in range(1, count + 1)]
    largest = reach if full else min(reach, max(-(-total // count), total * weights[0] // sum(weights)))
    least = 1 if total - largest >= count - 1 else 0
    given, spare = [largest] + [least] * (count - 1), total - largest - least * (count - 1)
    while spare > 0:
        candidates = [i for i in range(1, count) if given[i] < largest] or [i for i in range(1, count) if given[i] < reach]
        mass, remaining = sum([weights[i] for i in candidates]), spare
        for i in candidates:
            addition = min(reach - given[i], max(1, remaining * weights[i] // mass), spare)
            given[i] = given[i] + addition
            spare = spare - addition
    return np.array(given)


def gaussian(own_key, shape, scale, limit, cuts=(), held_as=jnp.bfloat16):
    gain = steps_of(own_key, shape, cuts, -0.22, 0.18) if cuts else 1.0
    result = jax.random.normal(own_key, shape, jnp.float32) * scale * gain
    return jnp.minimum(jnp.maximum(result, -limit), limit).astype(held_as)


def bell_draw_with(own_key, shape, scale, limit, cuts, heavy, kind=jnp.bfloat16):
    values = scale * jax.random.normal(own_key, shape, jnp.float32)
    if cuts:
        values = values * steps_of(own_key, shape, cuts, -0.22, 0.18)
    return jnp.clip(with_spikes(values, jax.random.fold_in(own_key, 3), *heavy), -limit, limit).astype(kind)


def setup_inputs(seed: int = 0) -> dict:
    keys = jax.random.split(jax.random.key(seed), 11)
    tokens = bell_draw_with(keys[0], (TOKENS, D), 1.0, 24.0, ((0, 512),), (0, 1, 512, 6.0))
    out_grad = gaussian(keys[1], (TOKENS, D), 0.05, 0.29882812, ((0, 512),))
    gate_up = gaussian(keys[2], (TOKENS, TOPK, TWO_F), 1.5, 8.0, ((0, 512),))
    route_weight = jnp.clip(0.19921875 + 0.80078125 * jax.random.uniform(keys[3], (TOKENS, TOPK), jnp.float32) ** steps_of(keys[3], (TOKENS, TOPK), ((0, 512),), -0.2, 0.2), 0.19921875, 1.0).astype(jnp.bfloat16)
    routes_keys = jax.random.split(jax.random.fold_in(keys[4], 1), TOKENS // TOK_DEV)
    routes_turns = jax.random.permutation(jax.random.fold_in(keys[4], 3), TOKENS // TOK_DEV)
    routes = jax.vmap(lambda own, number: shared_out(jax.random.fold_in(keys[4], 2), own, number, TOK_DEV, EXPERTS, TOPK, CAP, 2))(routes_keys, routes_turns).reshape((TOKENS, TOPK))
    down_weight = gaussian(keys[5], (EXPERTS, F, D), F ** -0.5, 0.21875, ((0, 16), (1, 32)))
    master = gaussian(keys[6], (EXPERTS, BUCKETS, BCAP), 0.02, 0.12, ((0, 16), (1, 32)), jnp.float32)
    moment_one = gaussian(keys[7], (EXPERTS, BUCKETS, BCAP), 0.3, 2.0, ((0, 16), (1, 32)), jnp.float32)
    moment_two = jnp.clip(jnp.exp(math.log(5.0) - 4.6051702 * jax.random.uniform(keys[8], (EXPERTS, BUCKETS, BCAP), jnp.float32) ** steps_of(keys[8], (EXPERTS, BUCKETS, BCAP), ((0, 16), (1, 32)), -0.2, 0.2)), 0.05, 5.0)
    offsets = draw_offsets(jax.random.fold_in(keys[10], 71), 0)
    return {"tokens": tokens, "out_grad": out_grad, "gate_up": gate_up, "route_weight": route_weight, "routes": routes, "down_weight": down_weight, "master": master, "moment_one": moment_one, "moment_two": moment_two, "offsets": offsets}


beta_one = 0.9
beta_two = 0.95
learn_rate = 0.001
decay_rate = 0.1
adam_eps = 1e-08
adam_step = 20.0

def slab_terms(slab_tokens, slab_grads, slab_saved, slab_weight, slab_routes, down_weight):
    row_limit = N_EXPERT * CAP
    row_total = slab_routes.shape[0]

    def per_expert(expert):
        hits = slab_routes == expert
        order = jnp.argsort(jnp.where(hits, 0, 1).astype(jnp.int32), stable=True).astype(jnp.int32)
        picked = order[:row_limit]
        in_use = jnp.arange(row_limit, dtype=jnp.int32) < jnp.sum(hits.astype(jnp.int32))
        token_of = (picked // TOPK).astype(jnp.int32)
        features = slab_tokens[token_of]
        cotangent = jnp.where(in_use[:, None], slab_grads[token_of], jnp.zeros((), slab_grads.dtype))
        saved_gu = jnp.where(in_use[:, None], slab_saved[picked], jnp.zeros((), slab_saved.dtype))
        weight_row = jnp.where(in_use, slab_weight[picked].astype(jnp.float32), jnp.float32(0.0))
        back_prod = jnp.dot(cotangent, down_weight[expert].T, preferred_element_type=jnp.float32)
        gate_pre = saved_gu[:, :F].astype(jnp.float32)
        up_part = saved_gu[:, F:].astype(jnp.float32)
        sigmoid_gate = jax.nn.sigmoid(gate_pre)
        activation = gate_pre * sigmoid_gate * up_part
        scores = lax.optimization_barrier(jnp.sum(activation * back_prod, axis=1))
        scaled = weight_row[:, None] * back_prod
        grad_gate = scaled * up_part * sigmoid_gate * (1.0 + gate_pre * (1.0 - sigmoid_gate))
        grad_up = scaled * gate_pre * sigmoid_gate
        grad_joined = jnp.concatenate([grad_gate, grad_up], axis=1).astype(jnp.bfloat16)
        partial_sum = jnp.dot(features.T, grad_joined, preferred_element_type=jnp.float32).astype(jnp.bfloat16)
        return (partial_sum, jnp.where(in_use, scores, jnp.float32(0.0)), picked)
    partials, scores, picked = lax.map(per_expert, jnp.arange(EXPERTS, dtype=jnp.int32))
    row_scores = jnp.zeros((row_total,), jnp.float32).at[picked.reshape(-1)].add(scores.reshape(-1))
    return (partials, row_scores)

def reference(tokens, out_grad, gate_up, route_weight, routes, down_weight, master, moment_one, moment_two, offsets):
    slab_tokens = N_EXPERT * TOK_DEV
    token_slabs = tokens.reshape(N_DP, slab_tokens, D)
    grad_slabs = out_grad.reshape(N_DP, slab_tokens, D)
    saved_slabs = gate_up.reshape(N_DP, slab_tokens * TOPK, 2 * F)
    weight_slabs = route_weight.reshape(N_DP, slab_tokens * TOPK)
    route_slabs = routes.reshape(N_DP, slab_tokens * TOPK)

    def add_slab(running, pieces):
        partials, row_scores = slab_terms(pieces[0], pieces[1], pieces[2], pieces[3], pieces[4], down_weight)
        return (running + partials.astype(jnp.float32), row_scores)
    grad_sum, all_scores = lax.scan(add_slab, jnp.zeros((EXPERTS, D, 2 * F), jnp.float32), (token_slabs, grad_slabs, saved_slabs, weight_slabs, route_slabs))
    router_grad = all_scores.reshape(TOKENS, TOPK)
    flat_size = D * 2 * F
    flat_grad = jnp.concatenate([grad_sum.reshape(EXPERTS, flat_size), jnp.zeros((EXPERTS, BCAP), jnp.float32)], axis=1)
    slot_ids = jnp.arange(BCAP, dtype=jnp.int32)
    bucket_len = (offsets[1:] - offsets[:-1]).astype(jnp.int32)
    in_bucket = slot_ids[None, :] < bucket_len[:, None]
    flat_index = (offsets[:-1, None] + slot_ids[None, :]).astype(jnp.int32)
    bucket_grad = jnp.where(in_bucket[None], flat_grad[:, flat_index], jnp.float32(0.0))
    moment_new = beta_one * moment_one + (1.0 - beta_one) * bucket_grad
    square_new = beta_two * moment_two + (1.0 - beta_two) * bucket_grad * bucket_grad
    update = moment_new / (1.0 - beta_one ** adam_step) / (jnp.sqrt(square_new / (1.0 - beta_two ** adam_step)) + adam_eps)
    master_new = master - learn_rate * (update + decay_rate * master)
    new_master = jnp.where(in_bucket[None], master_new, jnp.float32(0.0))
    new_moment_one = jnp.where(in_bucket[None], moment_new, jnp.float32(0.0))
    new_moment_two = jnp.where(in_bucket[None], square_new, jnp.float32(0.0))
    flat_pos = jnp.arange(flat_size, dtype=jnp.int32)
    owner = (jnp.searchsorted(offsets, flat_pos, side='right') - 1).astype(jnp.int32)
    owner = jnp.clip(owner, 0, N_DP - 1).astype(jnp.int32)
    inside = (flat_pos - offsets[owner]).astype(jnp.int32)
    new_weight = new_master[:, owner, inside].astype(jnp.bfloat16).reshape(EXPERTS, D, 2 * F)
    return (new_master, new_moment_one, new_moment_two, new_weight, router_grad)
```

```python
import functools

import jax
import jax.numpy as jnp
from jax import lax
from jax.experimental import pallas as pl
from jax.experimental.pallas import tpu as pltpu
from jax.sharding import PartitionSpec as P

beta_one = 0.9
beta_two = 0.95
learn_rate = 0.001
decay_rate = 0.1
adam_eps = 1e-08
adam_step = 20.0

MESH = pl.DeviceIdType.MESH


def sum_kernel(
    n,
    feat_ref,
    dgu_ref,
    out_ref,
    tail_ref,
    feat_t,
    own,
    give,
    sib,
    work,
    tail_in,
    sib_send,
    sib_recv,
    ring_send,
    ring_recv,
    tail_send,
    tail_recv,
):
    half = n // 2
    rows, width = out_ref.shape
    cols = width // 2
    dp = lax.axis_index("dp")
    expert = lax.axis_index("expert")
    z, c = dp // 2, dp % 2
    other = (z * 2 + 1 - c, expert)
    ahead = (lax.rem(z + 1, n) * 2 + c, expert)
    behind = (lax.rem(z + n - 1, n) * 2 + c, expert)
    upper = (lax.rem(dp + 1, 2 * n), expert)
    lower = (lax.rem(dp + 2 * n - 1, 2 * n), expert)

    barrier = pltpu.get_barrier_semaphore()
    for peer in (other, ahead, behind, upper, lower):
        pl.semaphore_signal(barrier, inc=1, device_id=peer, device_id_type=MESH)

    depth = feat_ref.shape[1]
    for i in range(depth // 256):
        feat_t[pl.ds(i * 256, 256), :] = feat_ref[:, pl.ds(i * 256, 256)].T

    def sib_copy(r):
        return pltpu.make_async_remote_copy(
            src_ref=give.at[r],
            dst_ref=sib.at[r],
            send_sem=sib_send.at[r],
            recv_sem=sib_recv.at[r],
            device_id=other,
            device_id_type=MESH,
        )

    def ring_copy(d, u, s):
        return pltpu.make_async_remote_copy(
            src_ref=work.at[d, u, s],
            dst_ref=work.at[d, u, s + 1],
            send_sem=ring_send.at[d, u, s],
            recv_sem=ring_recv.at[d, u, s],
            device_id=(ahead, behind)[d],
            device_id_type=MESH,
        )

    def produce(places):
        pieces = []
        for r in places:
            owner = lax.rem(z + r, n)
            for side in (c, 1 - c):
                start = pl.multiple_of((owner * 2 + side) * rows, 16)
                pieces.append(feat_t[pl.ds(start, rows), :])
        lhs = jnp.concatenate(pieces, axis=0)
        for j in range(width // 256):
            at = pl.ds(j * 256, 256)
            prod = jnp.dot(lhs, dgu_ref[:, at], preferred_element_type=jnp.float32)
            prod = prod.astype(jnp.bfloat16)
            for i, r in enumerate(places):
                own[r, :, at] = prod[2 * i * rows : (2 * i + 1) * rows]
                give[r, :, at] = prod[(2 * i + 1) * rows : (2 * i + 2) * rows]

    def chip_sum(r, u):
        at = pl.ds(u * cols, cols)
        return own[r, :, at].astype(jnp.float32) + sib[r, :, at].astype(jnp.float32)

    def step(s, streams, fresh):
        k = half - s
        for d, u in streams:
            r = k if d == 0 else n - k
            total = chip_sum(r, u)
            if (d, u) not in fresh:
                ring_copy(d, u, s - 1).wait_recv()
                total = total + work[d, u, s]
            work[d, u, s] = total
            ring_copy(d, u, s).start()

    every = ((0, 0), (1, 1), (0, 1), (1, 0))
    produce([half])
    pl.semaphore_wait(barrier, 5)
    sib_copy(half).start()
    produce([half - 1, half + 1])
    sib_copy(half - 1).start()
    sib_copy(half + 1).start()
    sib_copy(half).wait_recv()
    step(0, every[:2], every[:2])

    def body(s, _):
        k = half - s
        sib_copy(k).wait_recv()
        sib_copy(n - k).wait_recv()

        @pl.when(s == 1)
        def _():
            step(s, every, every[2:])

        @pl.when(s > 1)
        def _():
            step(s, every, ())

        @pl.when(k > 1)
        def _():
            produce([k - 1, n - k + 1])
            sib_copy(k - 1).start()
            sib_copy(n - k + 1).start()

        return 0

    lax.fori_loop(1, half, body, 0)
    produce([0])
    sib_copy(0).start()
    sib_copy(0).wait_recv()
    for u in range(2):
        ring_copy(0, u, half - 1).wait_recv()
        ring_copy(1, u, half - 1).wait_recv()
        out_ref[:, pl.ds(u * cols, cols)] = chip_sum(0, u) + (work[0, u, half] + work[1, u, half])
    last = pltpu.make_async_remote_copy(
        src_ref=out_ref.at[pl.ds(rows - 8, 8)],
        dst_ref=tail_in,
        send_sem=tail_send,
        recv_sem=tail_recv,
        device_id=upper,
        device_id_type=MESH,
    )
    last.start()

    def drain(r, _):
        sib_copy(r).wait_send()
        return 0

    lax.fori_loop(0, n, drain, 0)

    def drain_ring(s, _):
        for d, u in every:
            ring_copy(d, u, s).wait_send()
        return 0

    for d, u in every[:2]:
        ring_copy(d, u, 0).wait_send()
    lax.fori_loop(1, half, drain_ring, 0)
    last.wait()
    tail_ref[...] = tail_in[...]


def sum_over_slabs(features, dgu, n):
    depth, width = features.shape[1], dgu.shape[1]
    rows = depth // (2 * n)
    half = n // 2
    dma = pltpu.SemaphoreType.DMA
    return pl.pallas_call(
        functools.partial(sum_kernel, n),
        out_shape=(
            jax.ShapeDtypeStruct((rows, width), jnp.float32),
            jax.ShapeDtypeStruct((8, width), jnp.float32),
        ),
        in_specs=[pl.BlockSpec(memory_space=pltpu.VMEM)] * 2,
        out_specs=[pl.BlockSpec(memory_space=pltpu.VMEM)] * 2,
        scratch_shapes=[
            pltpu.VMEM((depth, features.shape[0]), jnp.bfloat16),
            pltpu.VMEM((n, rows, width), jnp.bfloat16),
            pltpu.VMEM((n, rows, width), jnp.bfloat16),
            pltpu.VMEM((n, rows, width), jnp.bfloat16),
            pltpu.VMEM((2, 2, half + 1, rows, width // 2), jnp.float32),
            pltpu.VMEM((8, width), jnp.float32),
            dma((n,)),
            dma((n,)),
            dma((2, 2, half)),
            dma((2, 2, half)),
            dma,
            dma,
        ],
        compiler_params=pltpu.CompilerParams(
            collective_id=0, has_side_effects=True, vmem_limit_bytes=40 * 2**20
        ),
        cost_estimate=pl.CostEstimate(
            flops=2 * features.shape[0] * depth * width,
            bytes_accessed=4 * depth * width,
            transcendentals=0,
        ),
    )(features, dgu)


def shifted(block, axis, distance):
    devices = range(lax.axis_size(axis))
    route = [(i - distance, i) for i in devices if i - distance in devices]
    return lax.ppermute(block, axis, route)


def cut_window(source, from_index, window_len):
    return lax.dynamic_slice_in_dim(source, from_index, window_len, 1)


def zero_cols(row_count, col_count, kind):
    return jnp.zeros((row_count, col_count), kind)


def shards(
    tokens,
    out_grad,
    gate_up,
    route_weight,
    routes,
    down_weight,
    master,
    moment_one,
    moment_two,
    offsets,
):
    token_count, model_width = tokens.shape
    choice_count = routes.shape[1]
    hidden = gate_up.shape[2] // 2
    local_experts = master.shape[0]
    bucket_cap = master.shape[2]
    groups = lax.axis_size("expert")
    dp_count = lax.axis_size("dp")
    experts = groups * local_experts
    row_count = token_count * choice_count
    capacity = 2 * row_count // experts
    row_expert = routes.reshape(row_count)
    onehot = (row_expert[:, None] == jnp.arange(experts, dtype=jnp.int32)[None, :]).astype(
        jnp.int32
    )
    earlier = jnp.cumsum(onehot, axis=0) - onehot
    row_slot = jnp.sum(earlier * onehot, axis=1)
    target = jnp.arange(experts * capacity, dtype=jnp.int32)
    select = (
        (row_expert[None, :] == target[:, None] // capacity)
        & (row_slot[None, :] == target[:, None] % capacity)
    ).astype(jnp.bfloat16)
    row_tokens = jnp.repeat(tokens, choice_count, axis=0)
    row_grads = jnp.repeat(out_grad, choice_count, axis=0)
    payload = jnp.concatenate(
        [row_tokens, row_grads, gate_up.reshape(row_count, 2 * hidden)], axis=1
    )
    packed = jnp.dot(select, payload, preferred_element_type=jnp.float32).astype(jnp.bfloat16)
    packed = packed.reshape(experts, capacity, payload.shape[1])
    weight_sent = jnp.dot(select, route_weight, preferred_element_type=jnp.float32)
    weight_sent = weight_sent.reshape(experts, capacity).astype(jnp.bfloat16)
    arrived, arrived_weight = (
        lax.all_to_all(packed, "expert", split_axis=0, concat_axis=1, tiled=True),
        lax.all_to_all(weight_sent, "expert", split_axis=0, concat_axis=1, tiled=True),
    )
    features = arrived[:, :, :model_width]
    cotangent = arrived[:, :, model_width : 2 * model_width]
    saved_gu = arrived[:, :, 2 * model_width :]
    back_prod = jnp.einsum(
        "lrd,lkd->lrk",
        cotangent,
        lax.all_gather(down_weight, "dp", axis=1, tiled=True),
        preferred_element_type=jnp.float32,
    )
    gate_pre = saved_gu[:, :, :hidden].astype(jnp.float32)
    up_part = saved_gu[:, :, hidden:].astype(jnp.float32)
    sigmoid_gate = jax.nn.sigmoid(gate_pre)
    activation = gate_pre * sigmoid_gate * up_part
    scores = jnp.sum(activation * back_prod, axis=2)
    scaled = arrived_weight.astype(jnp.float32)[:, :, None] * back_prod
    grad_gate = scaled * up_part * sigmoid_gate * (1.0 + gate_pre * (1.0 - sigmoid_gate))
    grad_up = scaled * gate_pre * sigmoid_gate
    grad_joined = jnp.concatenate([grad_gate, grad_up], axis=2).astype(jnp.bfloat16)
    row_block, below_rows = sum_over_slabs(features[0], grad_joined[0], dp_count // 2)
    returned = lax.all_to_all(scores, "expert", split_axis=1, concat_axis=0, tiled=True)
    flat_scores = returned.reshape(experts * capacity)
    router_grad = jnp.take(flat_scores, row_expert * capacity + row_slot).reshape(
        token_count, choice_count
    )
    flat_size = model_width * 2 * hidden
    even_size = flat_size // dp_count
    margin_size = bucket_cap - even_size
    position = lax.axis_index("dp")
    start_at = offsets[position]
    finish = offsets[position + 1]
    bucket_len = finish - start_at
    lead_shift = start_at - position * even_size
    tail_shift = finish - (position + 1) * even_size
    slot_ids = jnp.arange(bucket_cap, dtype=jnp.int32)
    in_bucket = slot_ids < bucket_len
    row_sum = row_block.reshape(1, even_size)
    from_below = below_rows.reshape(1, -1)[:, -margin_size:]
    extended = jnp.concatenate(
        [from_below, row_sum, zero_cols(local_experts, margin_size, jnp.float32)], axis=1
    )
    bucket_grad = cut_window(extended, lead_shift + margin_size, bucket_cap)
    bucket_grad = jnp.where(in_bucket[None, :], bucket_grad, 0.0)
    old_master = master[:, 0, :]
    moment_new = beta_one * moment_one[:, 0, :] + (1.0 - beta_one) * bucket_grad
    square_new = beta_two * moment_two[:, 0, :] + (1.0 - beta_two) * bucket_grad * bucket_grad
    update = (
        moment_new
        / (1.0 - beta_one**adam_step)
        / (jnp.sqrt(square_new / (1.0 - beta_two**adam_step)) + adam_eps)
    )
    master_new = old_master - learn_rate * (update + decay_rate * old_master)
    new_master = jnp.where(in_bucket[None, :], master_new, 0.0)
    new_moment_one = jnp.where(in_bucket[None, :], moment_new, 0.0)
    new_moment_two = jnp.where(in_bucket[None, :], square_new, 0.0)
    weight_half = new_master.astype(jnp.bfloat16)
    head_part = weight_half[:, :margin_size]
    from_above = shifted(head_part, "dp", -1)
    from_own = cut_window(weight_half, -lead_shift, even_size)
    from_next = cut_window(
        jnp.concatenate([zero_cols(local_experts, even_size, jnp.bfloat16), from_above], axis=1),
        -tail_shift,
        even_size,
    )
    new_weight = (from_own + from_next).reshape(local_experts, model_width // dp_count, 2 * hidden)
    return (
        new_master[:, None, :],
        new_moment_one[:, None, :],
        new_moment_two[:, None, :],
        new_weight,
        router_grad,
    )


def solution(mesh):
    placed = (
        P(("dp", "expert"), None),
        P(("dp", "expert"), None),
        P(("dp", "expert"), None, None),
        P(("dp", "expert"), None),
        P(("dp", "expert"), None),
        P("expert", "dp", None),
        P("expert", "dp", None),
        P("expert", "dp", None),
        P("expert", "dp", None),
        P(),
    )
    return jax.shard_map(
        shards,
        mesh=mesh,
        in_specs=placed,
        out_specs=(
            P("expert", "dp", None),
            P("expert", "dp", None),
            P("expert", "dp", None),
            P("expert", "dp", None),
            P(("dp", "expert"), None),
        ),
        check_vma=False,
    )
```

```python
import functools

import jax
import jax.numpy as jnp
from jax import lax
from jax.experimental import pallas as pl
from jax.experimental.pallas import tpu as pltpu
from jax.sharding import PartitionSpec as P

beta_one = 0.9
beta_two = 0.95
learn_rate = 0.001
decay_rate = 0.1
adam_eps = 1e-08
adam_step = 20.0

MESH = pl.DeviceIdType.MESH


def expert_peers(experts):
    side = 4 if experts % 4 == 0 else experts
    me = lax.axis_index("expert")

    def peer(i):
        x = lax.rem(me // side + i // side, experts // side)
        return x * side + lax.rem(me % side + i % side, side)

    return me, peer


def send_kernel(
    n,
    experts,
    tok_ref,
    grad_ref,
    saved_ref,
    weight_ref,
    route_ref,
    down_ref,
    feat_ref,
    dgu_ref,
    score_ref,
    target_ref,
    pack_one,
    pack_two,
    rows_in,
    down_wide,
    down_sib,
    down_all,
    one_send,
    one_recv,
    two_send,
    two_recv,
    ring_send,
    ring_recv,
    pass_send,
    pass_recv,
    first_send,
    first_recv,
):
    half = n // 2
    count, width = tok_ref.shape
    hidden = saved_ref.shape[1] // 2
    slots = feat_ref.shape[0] // experts
    share = down_ref.shape[0]
    cols = width // 2
    dp = lax.axis_index("dp")
    me, peer = expert_peers(experts)
    z, c = dp // 2, dp % 2
    other = (z * 2 + 1 - c, me)
    ahead = (lax.rem(z + 1, n) * 2 + c, me)
    behind = (lax.rem(z + n - 1, n) * 2 + c, me)

    barrier = pltpu.get_barrier_semaphore()
    for device in (other, ahead, behind):
        pl.semaphore_signal(barrier, inc=1, device_id=device, device_id_type=MESH)

    def greet(i, _):
        pl.semaphore_signal(barrier, inc=1, device_id=(dp, peer(i)), device_id_type=MESH)
        return 0

    lax.fori_loop(1, experts, greet, 0)
    down_wide[...] = down_ref[...].astype(jnp.float32)
    pl.semaphore_wait(barrier, experts + 2)

    first = pltpu.make_async_remote_copy(
        src_ref=down_wide.at[:, pl.ds(pl.multiple_of((1 - c) * cols, 128), cols)],
        dst_ref=down_sib,
        send_sem=first_send,
        recv_sem=first_recv,
        device_id=other,
        device_id_type=MESH,
    )
    first.start()

    def place(idx):
        return pl.ds(pl.multiple_of(lax.rem(idx + n, n) * 2 * share, 16), 2 * share)

    def ring_copy(d, s, split):
        idx = z - s if d == 0 else z + s
        at = pl.ds(d * (cols // 2), cols // 2) if split else pl.ds(0, cols)
        block = down_all.at[c, place(idx), at]
        return pltpu.make_async_remote_copy(
            src_ref=block,
            dst_ref=block,
            send_sem=ring_send.at[d, s],
            recv_sem=ring_recv.at[d, s],
            device_id=(ahead, behind)[d],
            device_id_type=MESH,
        )

    def arrival(d, s, split):
        idx = z - s - 1 if d == 0 else z + s + 1
        at = pl.ds(d * (cols // 2), cols // 2) if split else pl.ds(0, cols)
        block = down_all.at[c, place(idx), at]
        return pltpu.make_async_remote_copy(
            src_ref=block,
            dst_ref=block,
            send_sem=ring_send.at[d, s],
            recv_sem=ring_recv.at[d, s],
            device_id=(ahead, behind)[d],
            device_id_type=MESH,
        )

    def pass_copy(r, side):
        block = down_all.at[side, place(z + r), pl.ds(0, cols)]
        return pltpu.make_async_remote_copy(
            src_ref=block,
            dst_ref=block,
            send_sem=pass_send.at[r],
            recv_sem=pass_recv.at[r],
            device_id=other,
            device_id_type=MESH,
        )

    route = route_ref[...]
    expert_id = lax.broadcasted_iota(jnp.int32, (experts, count), 0)
    onehot = jnp.where(route == expert_id, 1.0, 0.0)
    before = lax.broadcasted_iota(jnp.int32, (count, count), 0)
    after = lax.broadcasted_iota(jnp.int32, (count, count), 1)
    upper = jnp.where(before < after, 1.0, 0.0).astype(jnp.bfloat16)
    earlier = jnp.dot(onehot.astype(jnp.bfloat16), upper, preferred_element_type=jnp.float32)
    slot = jnp.sum(earlier * onehot, axis=0, keepdims=True).astype(jnp.int32)
    target = route * slots + slot
    target_ref[...] = target
    slot_id = lax.broadcasted_iota(jnp.int32, (experts * slots, count), 0)
    select = jnp.where(slot_id == target, 1.0, 0.0).astype(jnp.bfloat16)

    def pack(into, at, values):
        into[:, pl.ds(at, values.shape[1])] = jnp.dot(
            select, values, preferred_element_type=jnp.float32
        ).astype(jnp.bfloat16)

    def block(e):
        return pl.ds(pl.multiple_of(e * slots, 16), slots)

    def one_copy(i):
        return pltpu.make_async_remote_copy(
            src_ref=pack_one.at[block(peer(i))],
            dst_ref=rows_in.at[block(me)],
            send_sem=one_send.at[i],
            recv_sem=one_recv.at[i],
            device_id=(dp, peer(i)),
            device_id_type=MESH,
        )

    def two_copy(i):
        return pltpu.make_async_remote_copy(
            src_ref=pack_two.at[block(peer(i))],
            dst_ref=feat_ref.at[block(me)],
            send_sem=two_send.at[i],
            recv_sem=two_recv.at[i],
            device_id=(dp, peer(i)),
            device_id_type=MESH,
        )

    step = 256 if width % 256 == 0 else width
    for j in range(width // step):
        pack(pack_one, j * step, grad_ref[:, pl.ds(j * step, step)])
    for j in range(2 * hidden // 256):
        pack(pack_one, width + j * 256, saved_ref[:, pl.ds(j * 256, 256)])
    wide = jnp.broadcast_to(weight_ref[...].astype(jnp.float32), (count, 128))
    pack(pack_one, width + 2 * hidden, wide.astype(jnp.bfloat16))

    first.wait()
    mine = down_wide[:, pl.ds(pl.multiple_of(c * cols, 128), cols)]
    theirs = down_sib[...]
    top, low = jnp.where(c == 0, mine, theirs), jnp.where(c == 0, theirs, mine)
    down_all[c, place(z), :] = jnp.concatenate([top, low], axis=0).astype(jnp.bfloat16)
    ring_copy(0, 0, half == 1).start()
    ring_copy(1, 0, half == 1).start()

    def send_one(i, _):
        one_copy(i).start()
        return 0

    lax.fori_loop(1, experts, send_one, 0)
    pass_copy(0, c).start()
    for j in range(width // step):
        pack(pack_two, j * step, tok_ref[:, pl.ds(j * step, step)])

    def send_two(i, _):
        two_copy(i).start()
        return 0

    lax.fori_loop(1, experts, send_two, 0)
    rows_in[block(me), :] = pack_one[block(me), :]
    feat_ref[block(me), :] = pack_two[block(me), :]

    def forward(s, _):
        arrival(0, s - 1, False).wait_recv()
        arrival(1, s - 1, False).wait_recv()

        @pl.when(s < half - 1)
        def _():
            ring_copy(0, s, False).start()
            ring_copy(1, s, False).start()

        @pl.when(s == half - 1)
        def _():
            ring_copy(0, s, True).start()
            ring_copy(1, s, True).start()

        pass_copy(n - s, c).start()
        pass_copy(s, c).start()
        return 0

    lax.fori_loop(1, half, forward, 0)
    arrival(0, half - 1, True).wait_recv()
    arrival(1, half - 1, True).wait_recv()
    pass_copy(half, c).start()

    def land_one(i, _):
        one_copy(i).wait_recv()
        return 0

    lax.fori_loop(1, experts, land_one, 0)

    def land_pass(r, _):
        pass_copy(r, 1 - c).wait_recv()
        return 0

    lax.fori_loop(0, n, land_pass, 0)

    tile = 256 if hidden % 256 == 0 else hidden
    weight = rows_in[:, pl.ds(width + 2 * hidden, 128)].astype(jnp.float32)[:, :1]
    score = jnp.zeros((experts * slots, 1), jnp.float32)
    for j in range(hidden // tile):
        back = sum(
            lax.dot_general(
                rows_in[:, pl.ds(side * cols, cols)],
                down_all[side, pl.ds(j * tile, tile), :],
                (((1,), (1,)), ((), ())),
                preferred_element_type=jnp.float32,
            )
            for side in range(2)
        )
        gate = rows_in[:, pl.ds(width + j * tile, tile)].astype(jnp.float32)
        up = rows_in[:, pl.ds(width + hidden + j * tile, tile)].astype(jnp.float32)
        sig = 1.0 / (1.0 + jnp.exp(-gate))
        silu = gate * sig
        score = score + jnp.sum(silu * up * back, axis=1, keepdims=True)
        scaled = weight * back
        dgu_ref[:, pl.ds(j * tile, tile)] = (
            scaled * up * sig * (1.0 + gate * (1.0 - sig))
        ).astype(jnp.bfloat16)
        dgu_ref[:, pl.ds(hidden + j * tile, tile)] = (scaled * silu).astype(jnp.bfloat16)
    score_ref[...] = jnp.broadcast_to(score, score_ref.shape)

    def finish(i, _):
        one_copy(i).wait_send()
        two_copy(i).wait()
        return 0

    lax.fori_loop(1, experts, finish, 0)

    def finish_pass(r, _):
        pass_copy(r, c).wait_send()
        return 0

    lax.fori_loop(0, n, finish_pass, 0)

    def finish_ring(s, _):
        ring_copy(0, s, False).wait_send()
        ring_copy(1, s, False).wait_send()
        return 0

    lax.fori_loop(0, half - 1, finish_ring, 0)
    ring_copy(0, half - 1, True).wait_send()
    ring_copy(1, half - 1, True).wait_send()


def rows_to_experts(tokens, out_grad, saved, weight, routes, down, n, experts, slots):
    count, width = tokens.shape
    hidden = saved.shape[1] // 2
    total = experts * slots
    half = n // 2
    wide = width + 2 * hidden + 128
    dma = pltpu.SemaphoreType.DMA
    bf16, f32 = jnp.bfloat16, jnp.float32
    return pl.pallas_call(
        functools.partial(send_kernel, n, experts),
        out_shape=(
            jax.ShapeDtypeStruct((total, width), bf16),
            jax.ShapeDtypeStruct((total, 2 * hidden), bf16),
            jax.ShapeDtypeStruct((total, count), f32),
            jax.ShapeDtypeStruct((1, count), jnp.int32),
        ),
        in_specs=[pl.BlockSpec(memory_space=pltpu.VMEM)] * 6,
        out_specs=[pl.BlockSpec(memory_space=pltpu.VMEM)] * 4,
        scratch_shapes=[
            pltpu.VMEM((total, wide), bf16),
            pltpu.VMEM((total, width), bf16),
            pltpu.VMEM((total, wide), bf16),
            pltpu.VMEM(down.shape, f32),
            pltpu.VMEM((down.shape[0], width // 2), f32),
            pltpu.VMEM((2, hidden, width // 2), bf16),
            dma((experts,)),
            dma((experts,)),
            dma((experts,)),
            dma((experts,)),
            dma((2, half)),
            dma((2, half)),
            dma((n,)),
            dma((n,)),
            dma,
            dma,
        ],
        compiler_params=pltpu.CompilerParams(
            collective_id=1, has_side_effects=True, vmem_limit_bytes=32 * 2**20
        ),
        cost_estimate=pl.CostEstimate(
            flops=2 * total * (width * hidden + count * wide),
            bytes_accessed=4 * total * wide,
            transcendentals=total * hidden,
        ),
    )(tokens, out_grad, saved, weight, routes.reshape(1, count), down)


def sum_kernel(
    n,
    experts,
    feat_ref,
    dgu_ref,
    score_ref,
    target_ref,
    out_ref,
    tail_ref,
    router_ref,
    feat_t,
    own,
    give,
    sib,
    work,
    scale,
    tail_in,
    score_in,
    sib_send,
    sib_recv,
    ring_send,
    ring_recv,
    scale_send,
    scale_recv,
    score_send,
    score_recv,
    tail_send,
    tail_recv,
):
    half = n // 2
    rows, width = out_ref.shape
    cols = width // 2
    slots = score_ref.shape[0] // experts
    dp = lax.axis_index("dp")
    me, peer = expert_peers(experts)
    z, c = dp // 2, dp % 2
    other = (z * 2 + 1 - c, me)
    ahead = (lax.rem(z + 1, n) * 2 + c, me)
    behind = (lax.rem(z + n - 1, n) * 2 + c, me)
    upper = (lax.rem(dp + 1, 2 * n), me)
    lower = (lax.rem(dp + 2 * n - 1, 2 * n), me)

    barrier = pltpu.get_barrier_semaphore()
    for device in (other, ahead, behind, upper, lower):
        pl.semaphore_signal(barrier, inc=1, device_id=device, device_id_type=MESH)

    def greet(i, _):
        pl.semaphore_signal(barrier, inc=1, device_id=(dp, peer(i)), device_id_type=MESH)
        return 0

    lax.fori_loop(1, experts, greet, 0)

    depth = feat_ref.shape[1]
    for i in range(depth // 256):
        feat_t[pl.ds(i * 256, 256), :] = feat_ref[:, pl.ds(i * 256, 256)].T

    def score_copy(i):
        return pltpu.make_async_remote_copy(
            src_ref=score_ref.at[pl.ds(pl.multiple_of(peer(i) * slots, 8), slots)],
            dst_ref=score_in.at[pl.ds(pl.multiple_of(me * slots, 8), slots)],
            send_sem=score_send.at[i],
            recv_sem=score_recv.at[i],
            device_id=(dp, peer(i)),
            device_id_type=MESH,
        )

    def sib_copy(r):
        return pltpu.make_async_remote_copy(
            src_ref=give.at[r],
            dst_ref=sib.at[r],
            send_sem=sib_send.at[r],
            recv_sem=sib_recv.at[r],
            device_id=other,
            device_id_type=MESH,
        )

    def ring_copy(d, u, s):
        return [
            pltpu.make_async_remote_copy(
                src_ref=buffer.at[d, u, s],
                dst_ref=buffer.at[d, u, s + 1],
                send_sem=send.at[d, u, s],
                recv_sem=recv.at[d, u, s],
                device_id=(ahead, behind)[d],
                device_id_type=MESH,
            )
            for buffer, send, recv in (
                (work, ring_send, ring_recv),
                (scale, scale_send, scale_recv),
            )
        ]

    def produce(places):
        pieces = []
        for r in places:
            owner = lax.rem(z + r, n)
            for side in (c, 1 - c):
                start = pl.multiple_of((owner * 2 + side) * rows, 16)
                pieces.append(feat_t[pl.ds(start, rows), :])
        lhs = jnp.concatenate(pieces, axis=0)
        for j in range(width // 256):
            at = pl.ds(j * 256, 256)
            prod = jnp.dot(lhs, dgu_ref[:, at], preferred_element_type=jnp.float32)
            prod = prod.astype(jnp.bfloat16)
            for i, r in enumerate(places):
                own[r, :, at] = prod[2 * i * rows : (2 * i + 1) * rows]
                give[r, :, at] = prod[(2 * i + 1) * rows : (2 * i + 2) * rows]

    def chip_sum(r, u):
        at = pl.ds(u * cols, cols)
        return own[r, :, at].astype(jnp.float32) + sib[r, :, at].astype(jnp.float32)

    def decoded(d, u, s):
        return work[d, u, s].astype(jnp.int32).astype(jnp.float32) * scale[d, u, s]

    def step(s, streams, fresh):
        k = half - s
        for d, u in streams:
            r = k if d == 0 else n - k
            total = chip_sum(r, u)
            if (d, u) not in fresh:
                for copy in ring_copy(d, u, s - 1):
                    copy.wait_recv()
                total = total + decoded(d, u, s)
            most = jnp.maximum(jnp.max(jnp.abs(total), axis=0, keepdims=True), 1e-30)
            scale[d, u, s] = most * (1.0 / 32767.0)
            coded = jnp.round(total * (32767.0 / most))
            work[d, u, s] = coded.astype(jnp.int32).astype(jnp.int16)
            for copy in ring_copy(d, u, s):
                copy.start()

    every = ((0, 0), (1, 1), (0, 1), (1, 0))
    produce([half])
    pl.semaphore_wait(barrier, experts + 4)
    sib_copy(half).start()
    produce([half - 1, half + 1])
    sib_copy(half - 1).start()
    sib_copy(half + 1).start()
    sib_copy(half).wait_recv()
    step(0, every[:2], every[:2])

    def send_score(i, _):
        score_copy(i).start()
        return 0

    lax.fori_loop(1, experts, send_score, 0)
    mine = pl.ds(pl.multiple_of(me * slots, 8), slots)
    score_in[mine, :] = score_ref[mine, :]

    def body(s, _):
        k = half - s
        sib_copy(k).wait_recv()
        sib_copy(n - k).wait_recv()

        @pl.when(s == 1)
        def _():
            step(s, every, every[2:])

        @pl.when(s > 1)
        def _():
            step(s, every, ())

        @pl.when(k > 1)
        def _():
            produce([k - 1, n - k + 1])
            sib_copy(k - 1).start()
            sib_copy(n - k + 1).start()

        return 0

    lax.fori_loop(1, half, body, 0)
    produce([0])
    sib_copy(0).start()

    def land_score(i, _):
        score_copy(i).wait()
        return 0

    lax.fori_loop(1, experts, land_score, 0)
    slot_id = lax.broadcasted_iota(jnp.int32, score_in.shape, 0)
    router_ref[...] = jnp.sum(
        jnp.where(slot_id == target_ref[...], score_in[...], 0.0), axis=0, keepdims=True
    )
    sib_copy(0).wait_recv()
    for u in range(2):
        for d in range(2):
            for copy in ring_copy(d, u, half - 1):
                copy.wait_recv()
        out_ref[:, pl.ds(u * cols, cols)] = chip_sum(0, u) + (
            decoded(0, u, half) + decoded(1, u, half)
        )
    last = pltpu.make_async_remote_copy(
        src_ref=out_ref.at[pl.ds(rows - 8, 8)],
        dst_ref=tail_in,
        send_sem=tail_send,
        recv_sem=tail_recv,
        device_id=upper,
        device_id_type=MESH,
    )
    last.start()

    def drain(r, _):
        sib_copy(r).wait_send()
        return 0

    lax.fori_loop(0, n, drain, 0)

    def drain_ring(s, _):
        for d, u in every:
            for copy in ring_copy(d, u, s):
                copy.wait_send()
        return 0

    for d, u in every[:2]:
        for copy in ring_copy(d, u, 0):
            copy.wait_send()
    lax.fori_loop(1, half, drain_ring, 0)
    last.wait()
    tail_ref[...] = tail_in[...]


def sum_over_slabs(features, dgu, scores, targets, n, experts):
    depth, width = features.shape[1], dgu.shape[1]
    rows = depth // (2 * n)
    half = n // 2
    dma = pltpu.SemaphoreType.DMA
    return pl.pallas_call(
        functools.partial(sum_kernel, n, experts),
        out_shape=(
            jax.ShapeDtypeStruct((rows, width), jnp.float32),
            jax.ShapeDtypeStruct((8, width), jnp.float32),
            jax.ShapeDtypeStruct(targets.shape, jnp.float32),
        ),
        in_specs=[pl.BlockSpec(memory_space=pltpu.VMEM)] * 4,
        out_specs=[pl.BlockSpec(memory_space=pltpu.VMEM)] * 3,
        scratch_shapes=[
            pltpu.VMEM((depth, features.shape[0]), jnp.bfloat16),
            pltpu.VMEM((n, rows, width), jnp.bfloat16),
            pltpu.VMEM((n, rows, width), jnp.bfloat16),
            pltpu.VMEM((n, rows, width), jnp.bfloat16),
            pltpu.VMEM((2, 2, half + 1, rows, width // 2), jnp.int16),
            pltpu.VMEM((2, 2, half + 1, 1, width // 2), jnp.float32),
            pltpu.VMEM((8, width), jnp.float32),
            pltpu.VMEM(scores.shape, jnp.float32),
            dma((n,)),
            dma((n,)),
            dma((2, 2, half)),
            dma((2, 2, half)),
            dma((2, 2, half)),
            dma((2, 2, half)),
            dma((experts,)),
            dma((experts,)),
            dma,
            dma,
        ],
        compiler_params=pltpu.CompilerParams(
            collective_id=0, has_side_effects=True, vmem_limit_bytes=40 * 2**20
        ),
        cost_estimate=pl.CostEstimate(
            flops=2 * features.shape[0] * depth * width,
            bytes_accessed=4 * depth * width,
            transcendentals=0,
        ),
    )(features, dgu, scores, targets)


def shifted(block, axis, distance):
    devices = range(lax.axis_size(axis))
    route = [(i - distance, i) for i in devices if i - distance in devices]
    return lax.ppermute(block, axis, route)


def cut_window(source, from_index, window_len):
    return lax.dynamic_slice_in_dim(source, from_index, window_len, 1)


def zero_cols(row_count, col_count, kind):
    return jnp.zeros((row_count, col_count), kind)


def shards(
    tokens,
    out_grad,
    gate_up,
    route_weight,
    routes,
    down_weight,
    master,
    moment_one,
    moment_two,
    offsets,
):
    token_count, model_width = tokens.shape
    choice_count = routes.shape[1]
    hidden = gate_up.shape[2] // 2
    local_experts = master.shape[0]
    bucket_cap = master.shape[2]
    groups = lax.axis_size("expert")
    dp_count = lax.axis_size("dp")
    experts = groups * local_experts
    n = dp_count // 2
    row_count = token_count * choice_count
    capacity = 2 * row_count // experts
    features, grad_joined, scores, targets = rows_to_experts(
        tokens,
        out_grad,
        gate_up.reshape(row_count, 2 * hidden),
        route_weight,
        routes,
        down_weight[0],
        n,
        experts,
        capacity,
    )
    row_block, below_rows, router_row = sum_over_slabs(
        features, grad_joined, scores, targets, n, experts
    )
    router_grad = router_row.reshape(token_count, choice_count)
    flat_size = model_width * 2 * hidden
    even_size = flat_size // dp_count
    margin_size = bucket_cap - even_size
    position = lax.axis_index("dp")
    start_at = offsets[position]
    finish = offsets[position + 1]
    bucket_len = finish - start_at
    lead_shift = start_at - position * even_size
    tail_shift = finish - (position + 1) * even_size
    slot_ids = jnp.arange(bucket_cap, dtype=jnp.int32)
    in_bucket = slot_ids < bucket_len
    row_sum = row_block.reshape(1, even_size)
    from_below = below_rows.reshape(1, -1)[:, -margin_size:]
    extended = jnp.concatenate(
        [from_below, row_sum, zero_cols(local_experts, margin_size, jnp.float32)], axis=1
    )
    bucket_grad = cut_window(extended, lead_shift + margin_size, bucket_cap)
    bucket_grad = jnp.where(in_bucket[None, :], bucket_grad, 0.0)
    old_master = master[:, 0, :]
    moment_new = beta_one * moment_one[:, 0, :] + (1.0 - beta_one) * bucket_grad
    square_new = beta_two * moment_two[:, 0, :] + (1.0 - beta_two) * bucket_grad * bucket_grad
    update = (
        moment_new
        / (1.0 - beta_one**adam_step)
        / (jnp.sqrt(square_new / (1.0 - beta_two**adam_step)) + adam_eps)
    )
    master_new = old_master - learn_rate * (update + decay_rate * old_master)
    new_master = jnp.where(in_bucket[None, :], master_new, 0.0)
    new_moment_one = jnp.where(in_bucket[None, :], moment_new, 0.0)
    new_moment_two = jnp.where(in_bucket[None, :], square_new, 0.0)
    weight_half = new_master.astype(jnp.bfloat16)
    head_part = weight_half[:, :margin_size]
    from_above = shifted(head_part, "dp", -1)
    from_own = cut_window(weight_half, -lead_shift, even_size)
    from_next = cut_window(
        jnp.concatenate([zero_cols(local_experts, even_size, jnp.bfloat16), from_above], axis=1),
        -tail_shift,
        even_size,
    )
    new_weight = (from_own + from_next).reshape(local_experts, model_width // dp_count, 2 * hidden)
    return (
        new_master[:, None, :],
        new_moment_one[:, None, :],
        new_moment_two[:, None, :],
        new_weight,
        router_grad,
    )


def solution(mesh):
    placed = (
        P(("dp", "expert"), None),
        P(("dp", "expert"), None),
        P(("dp", "expert"), None, None),
        P(("dp", "expert"), None),
        P(("dp", "expert"), None),
        P("expert", "dp", None),
        P("expert", "dp", None),
        P("expert", "dp", None),
        P("expert", "dp", None),
        P(),
    )
    return jax.shard_map(
        shards,
        mesh=mesh,
        in_specs=placed,
        out_specs=(
            P("expert", "dp", None),
            P("expert", "dp", None),
            P("expert", "dp", None),
            P("expert", "dp", None),
            P(("dp", "expert"), None),
        ),
        check_vma=False,
    )
```

```python
import functools

import jax
import jax.numpy as jnp
from jax import lax
from jax.experimental import pallas as pl
from jax.experimental.pallas import tpu as pltpu
from jax.sharding import PartitionSpec as P

beta_one = 0.9
beta_two = 0.95
learn_rate = 0.001
decay_rate = 0.1
adam_eps = 1e-08
adam_step = 20.0

MESH = pl.DeviceIdType.MESH


ONE_CUTS = 3
TWO_CUTS = 2


def distance(i, side):
    dx, dy = i // side, i % side
    return min(dx, 4 - dx) + min(dy, side - dy), -min(dx, 4 - dx), -min(i, 16 - i)


def grad_kernel(
    n,
    experts,
    tok_ref,
    grad_ref,
    saved_ref,
    weight_ref,
    route_ref,
    down_ref,
    out_ref,
    tail_ref,
    router_ref,
    tok_in,
    grad_in,
    saved_in,
    down_in,
    pack_one,
    pack_two,
    rows_in,
    feats,
    down_wide,
    down_sib,
    down_all,
    dgu,
    score,
    score_in,
    feat_t,
    own,
    give,
    sib,
    work,
    scale,
    tail_in,
    load_sem,
    one_send,
    one_recv,
    two_send,
    two_recv,
    ring_send,
    ring_recv,
    pass_send,
    pass_recv,
    first_send,
    first_recv,
    score_send,
    score_recv,
    sib_send,
    sib_recv,
    sum_send,
    sum_recv,
    scale_send,
    scale_recv,
    tail_send,
    tail_recv,
):
    half = n // 2
    count, depth = tok_ref.shape
    hidden = saved_ref.shape[1] // 2
    slots = rows_in.shape[0] // experts
    share = down_ref.shape[0]
    part = depth // 4
    rows, width = out_ref.shape
    cols = width // 2
    side = 4 if experts % 4 == 0 else experts
    dp = lax.axis_index("dp")
    me = lax.axis_index("expert")
    z, c = dp // 2, dp % 2
    other = (z * 2 + 1 - c, me)
    ahead = (lax.rem(z + 1, n) * 2 + c, me)
    behind = (lax.rem(z + n - 1, n) * 2 + c, me)
    upper = (lax.rem(dp + 1, 2 * n), me)
    lower = (lax.rem(dp + 2 * n - 1, 2 * n), me)
    every = ((0, 0), (1, 1), (0, 1), (1, 0))

    def peer_at(dx, dy):
        x = lax.rem(me // side + dx + 4 * side, experts // side)
        return x * side + lax.rem(me % side + dy + 4 * side, side)

    def peer(i):
        return peer_at(i // side, i % side)

    far = sorted(range(1, experts), key=lambda i: distance(i, side), reverse=True)

    def remote(source, target, send, recv, device):
        return pltpu.make_async_remote_copy(
            src_ref=source,
            dst_ref=target,
            send_sem=send,
            recv_sem=recv,
            device_id=device,
            device_id_type=MESH,
        )

    barrier = pltpu.get_barrier_semaphore()
    for device in (other, ahead, behind, upper, lower):
        pl.semaphore_signal(barrier, inc=1, device_id=device, device_id_type=MESH)

    def greet(i, _):
        pl.semaphore_signal(barrier, inc=1, device_id=(dp, peer(i)), device_id_type=MESH)
        return 0

    lax.fori_loop(1, experts, greet, 0)

    loads = [
        pltpu.make_async_copy(source, target, load_sem.at[i])
        for i, (source, target) in enumerate(
            ((down_ref, down_in), (grad_ref, grad_in), (saved_ref, saved_in), (tok_ref, tok_in))
        )
    ]
    for load in loads:
        load.start()

    first = remote(
        down_wide.at[:, pl.ds(pl.multiple_of((1 - c) * 2 * part, 128), 2 * part)],
        down_sib,
        first_send,
        first_recv,
        other,
    )

    def place(idx):
        return pl.ds(pl.multiple_of(lax.rem(idx + n, n) * 2 * share, 16), 2 * share)

    def down_copy(d, u, s):
        block = down_all.at[c, place(z - s if d == 0 else z + s), pl.ds(u * part, part)]
        return remote(
            block, block, ring_send.at[d, u, s], ring_recv.at[d, u, s], (ahead, behind)[d]
        )

    def pass_copy(r, half_at):
        block = down_all.at[half_at, place(z + r)]
        return remote(block, block, pass_send.at[r], pass_recv.at[r], other)

    route = route_ref[...]
    expert_id = lax.broadcasted_iota(jnp.int32, (experts, count), 0)
    onehot = jnp.where(route == expert_id, 1.0, 0.0)
    before = lax.broadcasted_iota(jnp.int32, (count, count), 0)
    after = lax.broadcasted_iota(jnp.int32, (count, count), 1)
    ahead_of = jnp.where(before < after, 1.0, 0.0).astype(jnp.bfloat16)
    earlier = jnp.dot(onehot.astype(jnp.bfloat16), ahead_of, preferred_element_type=jnp.float32)
    slot = jnp.sum(earlier * onehot, axis=0, keepdims=True).astype(jnp.int32)
    target = route * slots + slot
    slot_id = lax.broadcasted_iota(jnp.int32, (experts * slots, count), 0)
    chosen = jnp.where(slot_id == target, 1.0, 0.0)
    select = chosen.astype(jnp.bfloat16)
    slot_weight = jnp.sum(chosen * weight_ref[...].astype(jnp.float32), axis=1, keepdims=True)

    def pack(into, cuts, p, sources):
        size = into.shape[1] // cuts
        left = 0
        for source in sources:
            low, high = max(p * size, left), min((p + 1) * size, left + source.shape[1])
            if low < high:
                into[:, pl.ds(low, high - low)] = jnp.dot(
                    select,
                    source[:, pl.ds(low - left, high - low)],
                    preferred_element_type=jnp.float32,
                ).astype(jnp.bfloat16)
            left += source.shape[1]

    def block(e):
        return pl.ds(pl.multiple_of(e * slots, 16), slots)

    def one_copy(i, p):
        size = pack_one.shape[1] // ONE_CUTS
        at = pl.ds(pl.multiple_of(p * size, 128), size)
        return remote(
            pack_one.at[block(peer(i)), at],
            rows_in.at[block(me), at],
            one_send.at[i, p],
            one_recv.at[i, p],
            (dp, peer(i)),
        )

    def two_copy(i, p):
        size = pack_two.shape[1] // TWO_CUTS
        at = pl.ds(pl.multiple_of(p * size, 128), size)
        return remote(
            pack_two.at[block(peer(i)), at],
            feats.at[block(me), at],
            two_send.at[i, p],
            two_recv.at[i, p],
            (dp, peer(i)),
        )

    loads[0].wait()
    down_wide[...] = down_in[...].astype(jnp.float32)
    pl.semaphore_wait(barrier, experts + 4)
    first.start()
    pack_one[:, pl.ds(depth + 2 * hidden, 128)] = jnp.broadcast_to(
        slot_weight, (experts * slots, 128)
    ).astype(jnp.bfloat16)
    loads[1].wait()
    loads[2].wait()
    pack(pack_one, ONE_CUTS, 0, (grad_in, saved_in))
    for i in far:
        one_copy(i, 0).start()
    first.wait()
    mine = down_wide[:, pl.ds(pl.multiple_of(c * 2 * part, 128), 2 * part)]
    theirs = down_sib[...]
    top, low = jnp.where(c == 0, mine, theirs), jnp.where(c == 0, theirs, mine)
    down_all[c, place(z), :] = jnp.concatenate([top, low], axis=0).astype(jnp.bfloat16)
    for d, u in every:
        down_copy(d, u, 0).start()
    pass_copy(0, c).start()
    for p in range(1, ONE_CUTS):
        pack(pack_one, ONE_CUTS, p, (grad_in, saved_in))
        for i in far:
            one_copy(i, p).start()
    loads[3].wait()
    for p in range(TWO_CUTS):
        pack(pack_two, TWO_CUTS, p, (tok_in,))
        for i in far:
            two_copy(i, p).start()
    rows_in[block(me), :] = pack_one[block(me), :]
    feats[block(me), :] = pack_two[block(me), :]

    def forward(s, _):
        for d, u in every:
            down_copy(d, u, s - 1).wait_recv()
            if d == u:
                down_copy(d, u, s).start()
            else:

                @pl.when(s < half - 1)
                def _():
                    down_copy(d, u, s).start()

        pass_copy(n - s, c).start()
        pass_copy(s, c).start()
        return 0

    lax.fori_loop(1, half, forward, 0)
    for u in range(2):
        down_copy(u, u, half - 1).wait_recv()
    pass_copy(half, c).start()

    def land_one(i, _):
        for p in range(ONE_CUTS):
            one_copy(i, p).wait_recv()
        return 0

    lax.fori_loop(1, experts, land_one, 0)

    def land_pass(r, _):
        pass_copy(r, 1 - c).wait_recv()
        return 0

    lax.fori_loop(0, n, land_pass, 0)

    tile = 256
    weight = rows_in[:, pl.ds(depth + 2 * hidden, 128)].astype(jnp.float32)[:, :1]
    total = jnp.zeros((experts * slots, 1), jnp.float32)
    for j in range(hidden // tile):
        back = sum(
            lax.dot_general(
                rows_in[:, pl.ds(h * 2 * part, 2 * part)],
                down_all[h, pl.ds(j * tile, tile), :],
                (((1,), (1,)), ((), ())),
                preferred_element_type=jnp.float32,
            )
            for h in range(2)
        )
        gate = rows_in[:, pl.ds(depth + j * tile, tile)].astype(jnp.float32)
        up = rows_in[:, pl.ds(depth + hidden + j * tile, tile)].astype(jnp.float32)
        sig = 1.0 / (1.0 + jnp.exp(-gate))
        silu = gate * sig
        total = total + jnp.sum(silu * up * back, axis=1, keepdims=True)
        scaled = weight * back
        dgu[:, pl.ds(j * tile, tile)] = (
            scaled * up * sig * (1.0 + gate * (1.0 - sig))
        ).astype(jnp.bfloat16)
        dgu[:, pl.ds(hidden + j * tile, tile)] = (scaled * silu).astype(jnp.bfloat16)
    score[...] = jnp.broadcast_to(total, score.shape)

    def score_copy(i):
        return remote(
            score.at[pl.ds(pl.multiple_of(peer(i) * slots, 8), slots)],
            score_in.at[pl.ds(pl.multiple_of(me * slots, 8), slots)],
            score_send.at[i],
            score_recv.at[i],
            (dp, peer(i)),
        )

    def land_two(i, _):
        for p in range(TWO_CUTS):
            two_copy(i, p).wait_recv()
        return 0

    lax.fori_loop(1, experts, land_two, 0)
    for i in range(depth // 256):
        feat_t[pl.ds(i * 256, 256), :] = feats[:, pl.ds(i * 256, 256)].T

    def sib_copy(r):
        return remote(give.at[r], sib.at[r], sib_send.at[r], sib_recv.at[r], other)

    def ring_copy(d, u, s):
        return [
            remote(
                buffer.at[d, u, s],
                buffer.at[d, u, s + 1],
                send.at[d, u, s],
                recv.at[d, u, s],
                (ahead, behind)[d],
            )
            for buffer, send, recv in (
                (work, sum_send, sum_recv),
                (scale, scale_send, scale_recv),
            )
        ]

    def produce(places):
        pieces = []
        for r in places:
            owner = lax.rem(z + r, n)
            for core in (c, 1 - c):
                start = pl.multiple_of((owner * 2 + core) * rows, 16)
                pieces.append(feat_t[pl.ds(start, rows), :])
        lhs = jnp.concatenate(pieces, axis=0)
        for j in range(width // 256):
            at = pl.ds(j * 256, 256)
            prod = jnp.dot(lhs, dgu[:, at], preferred_element_type=jnp.float32)
            prod = prod.astype(jnp.bfloat16)
            for i, r in enumerate(places):
                own[r, :, at] = prod[2 * i * rows : (2 * i + 1) * rows]
                give[r, :, at] = prod[(2 * i + 1) * rows : (2 * i + 2) * rows]

    def chip_sum(r, u):
        at = pl.ds(u * cols, cols)
        return own[r, :, at].astype(jnp.float32) + sib[r, :, at].astype(jnp.float32)

    def decoded(d, u, s):
        return work[d, u, s].astype(jnp.int32).astype(jnp.float32) * scale[d, u, s]

    def step(s, streams, fresh):
        k = half - s
        for d, u in streams:
            r = k if d == 0 else n - k
            value = chip_sum(r, u)
            if (d, u) not in fresh:
                for copy in ring_copy(d, u, s - 1):
                    copy.wait_recv()
                value = value + decoded(d, u, s)
            most = jnp.maximum(jnp.max(jnp.abs(value), axis=0, keepdims=True), 1e-30)
            scale[d, u, s] = most * (1.0 / 32767.0)
            coded = jnp.round(value * (32767.0 / most))
            work[d, u, s] = coded.astype(jnp.int32).astype(jnp.int16)
            for copy in ring_copy(d, u, s):
                copy.start()

    produce([half])
    sib_copy(half).start()
    produce([half - 1, half + 1])
    sib_copy(half - 1).start()
    sib_copy(half + 1).start()
    sib_copy(half).wait_recv()
    step(0, every[:2], every[:2])

    def send_score(i, _):
        score_copy(i).start()
        return 0

    lax.fori_loop(1, experts, send_score, 0)
    mine_at = pl.ds(pl.multiple_of(me * slots, 8), slots)
    score_in[mine_at, :] = score[mine_at, :]

    def body(s, _):
        k = half - s
        sib_copy(k).wait_recv()
        sib_copy(n - k).wait_recv()

        @pl.when(s == 1)
        def _():
            step(s, every, every[2:])

        @pl.when(s > 1)
        def _():
            step(s, every, ())

        @pl.when(k > 1)
        def _():
            produce([k - 1, n - k + 1])
            sib_copy(k - 1).start()
            sib_copy(n - k + 1).start()

        return 0

    lax.fori_loop(1, half, body, 0)
    produce([0])
    sib_copy(0).start()

    def land_score(i, _):
        score_copy(i).wait()
        return 0

    lax.fori_loop(1, experts, land_score, 0)
    router_ref[...] = jnp.sum(chosen * score_in[...], axis=0, keepdims=True)

    def drain_one(i, _):
        for p in range(ONE_CUTS):
            one_copy(i, p).wait_send()
        for p in range(TWO_CUTS):
            two_copy(i, p).wait_send()
        return 0

    lax.fori_loop(1, experts, drain_one, 0)
    def drain_pass(r, _):
        pass_copy(r, c).wait_send()
        return 0

    lax.fori_loop(0, n, drain_pass, 0)

    def drain_down(s, _):
        for d, u in every:
            down_copy(d, u, s).wait_send()
        return 0

    lax.fori_loop(0, half - 1, drain_down, 0)
    for u in range(2):
        down_copy(u, u, half - 1).wait_send()

    def drain_sum(s, _):
        for d, u in every:
            for copy in ring_copy(d, u, s):
                copy.wait_send()
        return 0

    for d, u in every[:2]:
        for copy in ring_copy(d, u, 0):
            copy.wait_send()
    lax.fori_loop(1, half - 1, drain_sum, 0)
    sib_copy(0).wait_recv()
    for u in range(2):
        for d in range(2):
            for copy in ring_copy(d, u, half - 1):
                copy.wait_recv()
        out_ref[:, pl.ds(u * cols, cols)] = chip_sum(0, u) + (
            decoded(0, u, half) + decoded(1, u, half)
        )
    last = remote(out_ref.at[pl.ds(rows - 8, 8)], tail_in, tail_send, tail_recv, upper)
    last.start()

    def drain_sib(r, _):
        sib_copy(r).wait_send()
        return 0

    lax.fori_loop(0, n, drain_sib, 0)
    drain_sum(half - 1, 0)
    last.wait()
    tail_ref[...] = tail_in[...]


def weight_gradient(tokens, out_grad, saved, weight, routes, down, n, experts, slots):
    count, depth = tokens.shape
    hidden = saved.shape[1] // 2
    width = 2 * hidden
    total = experts * slots
    rows = depth // (2 * n)
    half = n // 2
    wide = depth + width + 128
    dma = pltpu.SemaphoreType.DMA
    bf16, f32 = jnp.bfloat16, jnp.float32
    anywhere = pl.BlockSpec(memory_space=pl.ANY)
    inside = pl.BlockSpec(memory_space=pltpu.VMEM)
    return pl.pallas_call(
        functools.partial(grad_kernel, n, experts),
        out_shape=(
            jax.ShapeDtypeStruct((rows, width), f32),
            jax.ShapeDtypeStruct((8, width), f32),
            jax.ShapeDtypeStruct((1, count), f32),
        ),
        in_specs=[anywhere, anywhere, anywhere, inside, inside, anywhere],
        out_specs=[inside] * 3,
        scratch_shapes=[
            pltpu.VMEM(tokens.shape, bf16),
            pltpu.VMEM(out_grad.shape, bf16),
            pltpu.VMEM(saved.shape, bf16),
            pltpu.VMEM(down.shape, bf16),
            pltpu.VMEM((total, wide), bf16),
            pltpu.VMEM((total, depth), bf16),
            pltpu.VMEM((total, wide), bf16),
            pltpu.VMEM((total, depth), bf16),
            pltpu.VMEM(down.shape, f32),
            pltpu.VMEM((down.shape[0], depth // 2), f32),
            pltpu.VMEM((2, hidden, depth // 2), bf16),
            pltpu.VMEM((total, width), bf16),
            pltpu.VMEM((total, count), f32),
            pltpu.VMEM((total, count), f32),
            pltpu.VMEM((depth, total), bf16),
            pltpu.VMEM((n, rows, width), bf16),
            pltpu.VMEM((n, rows, width), bf16),
            pltpu.VMEM((n, rows, width), bf16),
            pltpu.VMEM((2, 2, half + 1, rows, width // 2), jnp.int16),
            pltpu.VMEM((2, 2, half + 1, 1, width // 2), f32),
            pltpu.VMEM((8, width), f32),
            dma((4,)),
            dma((experts, ONE_CUTS)),
            dma((experts, ONE_CUTS)),
            dma((experts, TWO_CUTS)),
            dma((experts, TWO_CUTS)),
            dma((2, 2, half)),
            dma((2, 2, half)),
            dma((n,)),
            dma((n,)),
            dma,
            dma,
            dma((experts,)),
            dma((experts,)),
            dma((n,)),
            dma((n,)),
            dma((2, 2, half)),
            dma((2, 2, half)),
            dma((2, 2, half)),
            dma((2, 2, half)),
            dma,
            dma,
        ],
        compiler_params=pltpu.CompilerParams(
            collective_id=0, has_side_effects=True, vmem_limit_bytes=60 * 2**20
        ),
        cost_estimate=pl.CostEstimate(
            flops=2 * total * (depth * hidden + depth * width + count * wide),
            bytes_accessed=2 * count * wide,
            transcendentals=total * hidden,
        ),
    )(
        tokens,
        out_grad,
        saved,
        weight.reshape(1, count),
        routes.reshape(1, count),
        down,
    )


def shifted(block, axis, distance):
    devices = range(lax.axis_size(axis))
    route = [(i - distance, i) for i in devices if i - distance in devices]
    return lax.ppermute(block, axis, route)


def cut_window(source, from_index, window_len):
    return lax.dynamic_slice_in_dim(source, from_index, window_len, 1)


def zero_cols(row_count, col_count, kind):
    return jnp.zeros((row_count, col_count), kind)


def shards(
    tokens,
    out_grad,
    gate_up,
    route_weight,
    routes,
    down_weight,
    master,
    moment_one,
    moment_two,
    offsets,
):
    token_count, model_width = tokens.shape
    choice_count = routes.shape[1]
    hidden = gate_up.shape[2] // 2
    local_experts = master.shape[0]
    bucket_cap = master.shape[2]
    groups = lax.axis_size("expert")
    dp_count = lax.axis_size("dp")
    experts = groups * local_experts
    n = dp_count // 2
    row_count = token_count * choice_count
    capacity = 2 * row_count // experts
    row_block, below_rows, router_row = weight_gradient(
        tokens,
        out_grad,
        gate_up.reshape(row_count, 2 * hidden),
        route_weight,
        routes,
        down_weight[0],
        n,
        experts,
        capacity,
    )
    router_grad = router_row.reshape(token_count, choice_count)
    flat_size = model_width * 2 * hidden
    even_size = flat_size // dp_count
    margin_size = bucket_cap - even_size
    position = lax.axis_index("dp")
    start_at = offsets[position]
    finish = offsets[position + 1]
    bucket_len = finish - start_at
    lead_shift = start_at - position * even_size
    tail_shift = finish - (position + 1) * even_size
    slot_ids = jnp.arange(bucket_cap, dtype=jnp.int32)
    in_bucket = slot_ids < bucket_len
    row_sum = row_block.reshape(1, even_size)
    from_below = below_rows.reshape(1, -1)[:, -margin_size:]
    extended = jnp.concatenate(
        [from_below, row_sum, zero_cols(local_experts, margin_size, jnp.float32)], axis=1
    )
    bucket_grad = cut_window(extended, lead_shift + margin_size, bucket_cap)
    bucket_grad = jnp.where(in_bucket[None, :], bucket_grad, 0.0)
    old_master = master[:, 0, :]
    moment_new = beta_one * moment_one[:, 0, :] + (1.0 - beta_one) * bucket_grad
    square_new = beta_two * moment_two[:, 0, :] + (1.0 - beta_two) * bucket_grad * bucket_grad
    update = (
        moment_new
        / (1.0 - beta_one**adam_step)
        / (jnp.sqrt(square_new / (1.0 - beta_two**adam_step)) + adam_eps)
    )
    master_new = old_master - learn_rate * (update + decay_rate * old_master)
    new_master = jnp.where(in_bucket[None, :], master_new, 0.0)
    new_moment_one = jnp.where(in_bucket[None, :], moment_new, 0.0)
    new_moment_two = jnp.where(in_bucket[None, :], square_new, 0.0)
    weight_half = new_master.astype(jnp.bfloat16)
    head_part = weight_half[:, :margin_size]
    from_above = shifted(head_part, "dp", -1)
    from_own = cut_window(weight_half, -lead_shift, even_size)
    from_next = cut_window(
        jnp.concatenate([zero_cols(local_experts, even_size, jnp.bfloat16), from_above], axis=1),
        -tail_shift,
        even_size,
    )
    new_weight = (from_own + from_next).reshape(local_experts, model_width // dp_count, 2 * hidden)
    return (
        new_master[:, None, :],
        new_moment_one[:, None, :],
        new_moment_two[:, None, :],
        new_weight,
        router_grad,
    )


def solution(mesh):
    placed = (
        P(("dp", "expert"), None),
        P(("dp", "expert"), None),
        P(("dp", "expert"), None, None),
        P(("dp", "expert"), None),
        P(("dp", "expert"), None),
        P("expert", "dp", None),
        P("expert", "dp", None),
        P("expert", "dp", None),
        P("expert", "dp", None),
        P(),
    )
    return jax.shard_map(
        shards,
        mesh=mesh,
        in_specs=placed,
        out_specs=(
            P("expert", "dp", None),
            P("expert", "dp", None),
            P("expert", "dp", None),
            P("expert", "dp", None),
            P(("dp", "expert"), None),
        ),
        check_vma=False,
    )
```

```python
import functools

import jax
import jax.numpy as jnp
from jax import lax
from jax.experimental import pallas as pl
from jax.experimental.pallas import tpu as pltpu
from jax.sharding import PartitionSpec as P

beta_one = 0.9
beta_two = 0.95
learn_rate = 0.001
decay_rate = 0.1
adam_eps = 1e-08
adam_step = 20.0

MESH = pl.DeviceIdType.MESH


ONE_CUTS = 3
TWO_CUTS = 2


def distance(i, side):
    dx, dy = i // side, i % side
    return min(dx, 4 - dx) + min(dy, side - dy), -min(dx, 4 - dx), -min(i, 16 - i)


def grad_kernel(
    n,
    experts,
    tok_ref,
    grad_ref,
    saved_ref,
    weight_ref,
    route_ref,
    down_ref,
    master_ref,
    one_ref,
    two_ref,
    out_ref,
    tail_ref,
    router_ref,
    heads_ref,
    tok_in,
    grad_in,
    saved_in,
    down_in,
    pack_one,
    pack_two,
    rows_in,
    feats,
    down_wide,
    down_sib,
    down_all,
    dgu,
    score,
    score_in,
    feat_t,
    own,
    give,
    sib,
    work,
    scale,
    tail_in,
    heads_in,
    load_sem,
    one_send,
    one_recv,
    two_send,
    two_recv,
    ring_send,
    ring_recv,
    pass_send,
    pass_recv,
    first_send,
    first_recv,
    score_send,
    score_recv,
    sib_send,
    sib_recv,
    sum_send,
    sum_recv,
    scale_send,
    scale_recv,
    tail_send,
    tail_recv,
    head_send,
    head_recv,
):
    half = n // 2
    count, depth = tok_ref.shape
    hidden = saved_ref.shape[1] // 2
    slots = rows_in.shape[0] // experts
    share = down_ref.shape[0]
    part = depth // 4
    rows, width = out_ref.shape
    cols = width // 2
    side = 4 if experts % 4 == 0 else experts
    dp = lax.axis_index("dp")
    me = lax.axis_index("expert")
    z, c = dp // 2, dp % 2
    other = (z * 2 + 1 - c, me)
    ahead = (lax.rem(z + 1, n) * 2 + c, me)
    behind = (lax.rem(z + n - 1, n) * 2 + c, me)
    upper = (lax.rem(dp + 1, 2 * n), me)
    lower = (lax.rem(dp + 2 * n - 1, 2 * n), me)
    every = ((0, 0), (1, 1), (0, 1), (1, 0))

    def peer_at(dx, dy):
        x = lax.rem(me // side + dx + 4 * side, experts // side)
        return x * side + lax.rem(me % side + dy + 4 * side, side)

    def peer(i):
        return peer_at(i // side, i % side)

    far = sorted(range(1, experts), key=lambda i: distance(i, side), reverse=True)

    def remote(source, target, send, recv, device):
        return pltpu.make_async_remote_copy(
            src_ref=source,
            dst_ref=target,
            send_sem=send,
            recv_sem=recv,
            device_id=device,
            device_id_type=MESH,
        )

    barrier = pltpu.get_barrier_semaphore()
    for device in (other, ahead, behind, upper, lower):
        pl.semaphore_signal(barrier, inc=1, device_id=device, device_id_type=MESH)

    def greet(i, _):
        pl.semaphore_signal(barrier, inc=1, device_id=(dp, peer(i)), device_id_type=MESH)
        return 0

    lax.fori_loop(1, experts, greet, 0)

    loads = [
        pltpu.make_async_copy(source, target, load_sem.at[i])
        for i, (source, target) in enumerate(
            ((down_ref, down_in), (grad_ref, grad_in), (saved_ref, saved_in), (tok_ref, tok_in))
        )
    ]
    for load in loads:
        load.start()

    first = remote(
        down_wide.at[:, pl.ds(pl.multiple_of((1 - c) * 2 * part, 128), 2 * part)],
        down_sib,
        first_send,
        first_recv,
        other,
    )

    def place(idx):
        return pl.ds(pl.multiple_of(lax.rem(idx + n, n) * 2 * share, 16), 2 * share)

    def down_copy(d, u, s):
        block = down_all.at[c, place(z - s if d == 0 else z + s), pl.ds(u * part, part)]
        return remote(
            block, block, ring_send.at[d, u, s], ring_recv.at[d, u, s], (ahead, behind)[d]
        )

    def pass_copy(r, half_at):
        block = down_all.at[half_at, place(z + r)]
        return remote(block, block, pass_send.at[r], pass_recv.at[r], other)

    route = route_ref[...]
    expert_id = lax.broadcasted_iota(jnp.int32, (experts, count), 0)
    onehot = jnp.where(route == expert_id, 1.0, 0.0)
    before = lax.broadcasted_iota(jnp.int32, (count, count), 0)
    after = lax.broadcasted_iota(jnp.int32, (count, count), 1)
    ahead_of = jnp.where(before < after, 1.0, 0.0).astype(jnp.bfloat16)
    earlier = jnp.dot(onehot.astype(jnp.bfloat16), ahead_of, preferred_element_type=jnp.float32)
    slot = jnp.sum(earlier * onehot, axis=0, keepdims=True).astype(jnp.int32)
    target = route * slots + slot
    slot_id = lax.broadcasted_iota(jnp.int32, (experts * slots, count), 0)
    chosen = jnp.where(slot_id == target, 1.0, 0.0)
    select = chosen.astype(jnp.bfloat16)
    slot_weight = jnp.sum(chosen * weight_ref[...].astype(jnp.float32), axis=1, keepdims=True)

    def pack(into, cuts, p, sources):
        size = into.shape[1] // cuts
        left = 0
        for source in sources:
            low, high = max(p * size, left), min((p + 1) * size, left + source.shape[1])
            if low < high:
                into[:, pl.ds(low, high - low)] = jnp.dot(
                    select,
                    source[:, pl.ds(low - left, high - low)],
                    preferred_element_type=jnp.float32,
                ).astype(jnp.bfloat16)
            left += source.shape[1]

    def block(e):
        return pl.ds(pl.multiple_of(e * slots, 16), slots)

    def one_copy(i, p):
        size = pack_one.shape[1] // ONE_CUTS
        at = pl.ds(pl.multiple_of(p * size, 128), size)
        return remote(
            pack_one.at[block(peer(i)), at],
            rows_in.at[block(me), at],
            one_send.at[i, p],
            one_recv.at[i, p],
            (dp, peer(i)),
        )

    def two_copy(i, p):
        size = pack_two.shape[1] // TWO_CUTS
        at = pl.ds(pl.multiple_of(p * size, 128), size)
        return remote(
            pack_two.at[block(peer(i)), at],
            feats.at[block(me), at],
            two_send.at[i, p],
            two_recv.at[i, p],
            (dp, peer(i)),
        )

    def head_copy(i):
        source = (master_ref, one_ref, two_ref)[i]
        return remote(
            source.at[0, :, pl.ds(0, heads_in.shape[2])],
            heads_in.at[i],
            head_send.at[i],
            head_recv.at[i],
            lower,
        )

    loads[0].wait()
    down_wide[...] = down_in[...].astype(jnp.float32)
    pl.semaphore_wait(barrier, experts + 4)
    first.start()
    pack_one[:, pl.ds(depth + 2 * hidden, 128)] = jnp.broadcast_to(
        slot_weight, (experts * slots, 128)
    ).astype(jnp.bfloat16)
    loads[1].wait()
    loads[2].wait()
    pack(pack_one, ONE_CUTS, 0, (grad_in, saved_in))
    for i in far:
        one_copy(i, 0).start()
    first.wait()
    mine = down_wide[:, pl.ds(pl.multiple_of(c * 2 * part, 128), 2 * part)]
    theirs = down_sib[...]
    top, low = jnp.where(c == 0, mine, theirs), jnp.where(c == 0, theirs, mine)
    down_all[c, place(z), :] = jnp.concatenate([top, low], axis=0).astype(jnp.bfloat16)
    for d, u in every:
        down_copy(d, u, 0).start()
    pass_copy(0, c).start()
    for p in range(1, ONE_CUTS):
        pack(pack_one, ONE_CUTS, p, (grad_in, saved_in))
        for i in far:
            one_copy(i, p).start()
    loads[3].wait()
    for p in range(TWO_CUTS):
        pack(pack_two, TWO_CUTS, p, (tok_in,))
        for i in far:
            two_copy(i, p).start()
    for i in range(3):
        head_copy(i).start()
    rows_in[block(me), :] = pack_one[block(me), :]
    feats[block(me), :] = pack_two[block(me), :]

    def forward(s, _):
        for d, u in every:
            down_copy(d, u, s - 1).wait_recv()
            if d == u:
                down_copy(d, u, s).start()
            else:

                @pl.when(s < half - 1)
                def _():
                    down_copy(d, u, s).start()

        pass_copy(n - s, c).start()
        pass_copy(s, c).start()
        return 0

    lax.fori_loop(1, half, forward, 0)
    for u in range(2):
        down_copy(u, u, half - 1).wait_recv()
    pass_copy(half, c).start()

    def land_one(i, _):
        for p in range(ONE_CUTS):
            one_copy(i, p).wait_recv()
        return 0

    lax.fori_loop(1, experts, land_one, 0)

    def land_pass(r, _):
        pass_copy(r, 1 - c).wait_recv()
        return 0

    lax.fori_loop(0, n, land_pass, 0)

    tile = 256
    weight = rows_in[:, pl.ds(depth + 2 * hidden, 128)].astype(jnp.float32)[:, :1]
    total = jnp.zeros((experts * slots, 1), jnp.float32)
    for j in range(hidden // tile):
        back = sum(
            lax.dot_general(
                rows_in[:, pl.ds(h * 2 * part, 2 * part)],
                down_all[h, pl.ds(j * tile, tile), :],
                (((1,), (1,)), ((), ())),
                preferred_element_type=jnp.float32,
            )
            for h in range(2)
        )
        gate = rows_in[:, pl.ds(depth + j * tile, tile)].astype(jnp.float32)
        up = rows_in[:, pl.ds(depth + hidden + j * tile, tile)].astype(jnp.float32)
        sig = 1.0 / (1.0 + jnp.exp(-gate))
        silu = gate * sig
        total = total + jnp.sum(silu * up * back, axis=1, keepdims=True)
        scaled = weight * back
        dgu[:, pl.ds(j * tile, tile)] = (
            scaled * up * sig * (1.0 + gate * (1.0 - sig))
        ).astype(jnp.bfloat16)
        dgu[:, pl.ds(hidden + j * tile, tile)] = (scaled * silu).astype(jnp.bfloat16)
    score[...] = jnp.broadcast_to(total, score.shape)

    def score_copy(i):
        return remote(
            score.at[pl.ds(pl.multiple_of(peer(i) * slots, 8), slots)],
            score_in.at[pl.ds(pl.multiple_of(me * slots, 8), slots)],
            score_send.at[i],
            score_recv.at[i],
            (dp, peer(i)),
        )

    def land_two(i, _):
        for p in range(TWO_CUTS):
            two_copy(i, p).wait_recv()
        return 0

    lax.fori_loop(1, experts, land_two, 0)
    for i in range(depth // 256):
        feat_t[pl.ds(i * 256, 256), :] = feats[:, pl.ds(i * 256, 256)].T

    def sib_copy(r):
        return remote(give.at[r], sib.at[r], sib_send.at[r], sib_recv.at[r], other)

    def ring_copy(d, u, s):
        return [
            remote(
                buffer.at[d, u, s],
                buffer.at[d, u, s + 1],
                send.at[d, u, s],
                recv.at[d, u, s],
                (ahead, behind)[d],
            )
            for buffer, send, recv in (
                (work, sum_send, sum_recv),
                (scale, scale_send, scale_recv),
            )
        ]

    def produce(places):
        pieces = []
        for r in places:
            owner = lax.rem(z + r, n)
            for core in (c, 1 - c):
                start = pl.multiple_of((owner * 2 + core) * rows, 16)
                pieces.append(feat_t[pl.ds(start, rows), :])
        lhs = jnp.concatenate(pieces, axis=0)
        for j in range(width // 256):
            at = pl.ds(j * 256, 256)
            prod = jnp.dot(lhs, dgu[:, at], preferred_element_type=jnp.float32)
            prod = prod.astype(jnp.bfloat16)
            for i, r in enumerate(places):
                own[r, :, at] = prod[2 * i * rows : (2 * i + 1) * rows]
                give[r, :, at] = prod[(2 * i + 1) * rows : (2 * i + 2) * rows]

    def chip_sum(r, u):
        at = pl.ds(u * cols, cols)
        return own[r, :, at].astype(jnp.float32) + sib[r, :, at].astype(jnp.float32)

    def decoded(d, u, s):
        return work[d, u, s].astype(jnp.int32).astype(jnp.float32) * scale[d, u, s]

    def step(s, streams, fresh):
        k = half - s
        for d, u in streams:
            r = k if d == 0 else n - k
            value = chip_sum(r, u)
            if (d, u) not in fresh:
                for copy in ring_copy(d, u, s - 1):
                    copy.wait_recv()
                value = value + decoded(d, u, s)
            most = jnp.maximum(jnp.max(jnp.abs(value), axis=0, keepdims=True), 1e-30)
            scale[d, u, s] = most * (1.0 / 32767.0)
            coded = jnp.round(value * (32767.0 / most))
            work[d, u, s] = coded.astype(jnp.int32).astype(jnp.int16)
            for copy in ring_copy(d, u, s):
                copy.start()

    produce([half])
    sib_copy(half).start()
    produce([half - 1, half + 1])
    sib_copy(half - 1).start()
    sib_copy(half + 1).start()
    sib_copy(half).wait_recv()
    step(0, every[:2], every[:2])

    def send_score(i, _):
        score_copy(i).start()
        return 0

    lax.fori_loop(1, experts, send_score, 0)
    mine_at = pl.ds(pl.multiple_of(me * slots, 8), slots)
    score_in[mine_at, :] = score[mine_at, :]

    def body(s, _):
        k = half - s
        sib_copy(k).wait_recv()
        sib_copy(n - k).wait_recv()

        @pl.when(s == 1)
        def _():
            step(s, every, every[2:])

        @pl.when(s > 1)
        def _():
            step(s, every, ())

        @pl.when(k > 1)
        def _():
            produce([k - 1, n - k + 1])
            sib_copy(k - 1).start()
            sib_copy(n - k + 1).start()

        return 0

    lax.fori_loop(1, half, body, 0)
    produce([0])
    sib_copy(0).start()

    def land_score(i, _):
        score_copy(i).wait()
        return 0

    lax.fori_loop(1, experts, land_score, 0)
    router_ref[...] = jnp.sum(chosen * score_in[...], axis=0, keepdims=True)

    def drain_one(i, _):
        for p in range(ONE_CUTS):
            one_copy(i, p).wait_send()
        for p in range(TWO_CUTS):
            two_copy(i, p).wait_send()
        return 0

    lax.fori_loop(1, experts, drain_one, 0)
    for i in range(3):
        head_copy(i).wait()
    heads_ref[...] = heads_in[...]

    def drain_pass(r, _):
        pass_copy(r, c).wait_send()
        return 0

    lax.fori_loop(0, n, drain_pass, 0)

    def drain_down(s, _):
        for d, u in every:
            down_copy(d, u, s).wait_send()
        return 0

    lax.fori_loop(0, half - 1, drain_down, 0)
    for u in range(2):
        down_copy(u, u, half - 1).wait_send()

    def drain_sum(s, _):
        for d, u in every:
            for copy in ring_copy(d, u, s):
                copy.wait_send()
        return 0

    for d, u in every[:2]:
        for copy in ring_copy(d, u, 0):
            copy.wait_send()
    lax.fori_loop(1, half - 1, drain_sum, 0)
    sib_copy(0).wait_recv()
    for u in range(2):
        for d in range(2):
            for copy in ring_copy(d, u, half - 1):
                copy.wait_recv()
        out_ref[:, pl.ds(u * cols, cols)] = chip_sum(0, u) + (
            decoded(0, u, half) + decoded(1, u, half)
        )
    last = remote(out_ref.at[pl.ds(rows - 8, 8)], tail_in, tail_send, tail_recv, upper)
    last.start()

    def drain_sib(r, _):
        sib_copy(r).wait_send()
        return 0

    lax.fori_loop(0, n, drain_sib, 0)
    drain_sum(half - 1, 0)
    last.wait()
    tail_ref[...] = tail_in[...]


def weight_gradient(
    tokens, out_grad, saved, weight, routes, down, states, margin, n, experts, slots
):
    count, depth = tokens.shape
    hidden = saved.shape[1] // 2
    width = 2 * hidden
    total = experts * slots
    rows = depth // (2 * n)
    half = n // 2
    wide = depth + width + 128
    dma = pltpu.SemaphoreType.DMA
    bf16, f32 = jnp.bfloat16, jnp.float32
    anywhere = pl.BlockSpec(memory_space=pl.ANY)
    inside = pl.BlockSpec(memory_space=pltpu.VMEM)
    return pl.pallas_call(
        functools.partial(grad_kernel, n, experts),
        out_shape=(
            jax.ShapeDtypeStruct((rows, width), f32),
            jax.ShapeDtypeStruct((8, width), f32),
            jax.ShapeDtypeStruct((1, count), f32),
            jax.ShapeDtypeStruct((3, 1, margin), f32),
        ),
        in_specs=[anywhere, anywhere, anywhere, inside, inside] + [anywhere] * 4,
        out_specs=[inside] * 4,
        scratch_shapes=[
            pltpu.VMEM(tokens.shape, bf16),
            pltpu.VMEM(out_grad.shape, bf16),
            pltpu.VMEM(saved.shape, bf16),
            pltpu.VMEM(down.shape, bf16),
            pltpu.VMEM((total, wide), bf16),
            pltpu.VMEM((total, depth), bf16),
            pltpu.VMEM((total, wide), bf16),
            pltpu.VMEM((total, depth), bf16),
            pltpu.VMEM(down.shape, f32),
            pltpu.VMEM((down.shape[0], depth // 2), f32),
            pltpu.VMEM((2, hidden, depth // 2), bf16),
            pltpu.VMEM((total, width), bf16),
            pltpu.VMEM((total, count), f32),
            pltpu.VMEM((total, count), f32),
            pltpu.VMEM((depth, total), bf16),
            pltpu.VMEM((n, rows, width), bf16),
            pltpu.VMEM((n, rows, width), bf16),
            pltpu.VMEM((n, rows, width), bf16),
            pltpu.VMEM((2, 2, half + 1, rows, width // 2), jnp.int16),
            pltpu.VMEM((2, 2, half + 1, 1, width // 2), f32),
            pltpu.VMEM((8, width), f32),
            pltpu.VMEM((3, 1, margin), f32),
            dma((4,)),
            dma((experts, ONE_CUTS)),
            dma((experts, ONE_CUTS)),
            dma((experts, TWO_CUTS)),
            dma((experts, TWO_CUTS)),
            dma((2, 2, half)),
            dma((2, 2, half)),
            dma((n,)),
            dma((n,)),
            dma,
            dma,
            dma((experts,)),
            dma((experts,)),
            dma((n,)),
            dma((n,)),
            dma((2, 2, half)),
            dma((2, 2, half)),
            dma((2, 2, half)),
            dma((2, 2, half)),
            dma,
            dma,
            dma((3,)),
            dma((3,)),
        ],
        compiler_params=pltpu.CompilerParams(
            collective_id=0, has_side_effects=True, vmem_limit_bytes=60 * 2**20
        ),
        cost_estimate=pl.CostEstimate(
            flops=2 * total * (depth * hidden + depth * width + count * wide),
            bytes_accessed=2 * count * wide,
            transcendentals=total * hidden,
        ),
    )(
        tokens,
        out_grad,
        saved,
        weight.reshape(1, count),
        routes.reshape(1, count),
        down,
        *states,
    )


def shift_load(ref, offset, row, count):
    start, lead = offset // 128 + row, lax.rem(offset, 128)
    lane = lax.broadcasted_iota(jnp.int32, (count, 128), 1)
    turn = lax.rem(128 - lead, 128)
    this = pltpu.roll(ref[pl.ds(start, count), :], turn, 1)
    following = pltpu.roll(ref[pl.ds(start + 1, count), :], turn, 1)
    return jnp.where(lane < 128 - lead, this, following)


def adam(grad, master, moment_one, moment_two):
    moment_new = beta_one * moment_one + (1.0 - beta_one) * grad
    square_new = beta_two * moment_two + (1.0 - beta_two) * grad * grad
    update = (moment_new * (1.0 / (1.0 - beta_one**adam_step))) / (
        jnp.sqrt(square_new * (1.0 / (1.0 - beta_two**adam_step))) + adam_eps
    )
    return master - learn_rate * (update + decay_rate * master), moment_new, square_new


def step_kernel(
    place_ref,
    block_ref,
    below_ref,
    heads_ref,
    master_ref,
    one_ref,
    two_ref,
    new_master_ref,
    new_one_ref,
    new_two_ref,
    weight_ref,
    ext,
    states,
    made,
    flat,
    head_made,
    block,
    below,
    heads,
    in_sem,
    out_sem,
):
    lead, tail = place_ref[0], place_ref[1]
    rows, width = block_ref.shape
    lines = width // 128
    even = rows * lines
    slots = master_ref.shape[2] // 128
    extra = slots - even
    ahead = 8 * lines
    sources = (master_ref, one_ref, two_ref)
    results = (new_master_ref, new_one_ref, new_two_ref)
    pairs = [(block_ref, block), (below_ref, below)]
    for i in range(3):
        pairs.append((sources[i].reshape(slots, 128), states.at[i]))
        pairs.append((heads_ref.at[i].reshape(heads.shape[1], 128), heads.at[i]))
    loads = [pltpu.make_async_copy(*pair, in_sem.at[i]) for i, pair in enumerate(pairs)]
    for load in loads:
        load.start()
    for load in loads[:2]:
        load.wait()
    for g in range(lines):
        at = pl.ds(g * 128, 128)
        ext[pl.ds(g, 8, lines), :] = below[:, at]
        ext[pl.ds(ahead + g, rows, lines), :] = block[:, at]
    after = ahead + even
    ext[pl.ds(after, ext.shape[0] - after), :] = jnp.zeros((ext.shape[0] - after, 128), jnp.float32)
    held = even * 128 + tail - lead
    for load in loads[2:]:
        load.wait()

    def run(row, count):
        index = (
            (row + lax.broadcasted_iota(jnp.int32, (count, 128), 0)) * 128
            + lax.broadcasted_iota(jnp.int32, (count, 128), 1)
        )
        inside = index < held
        grad = jnp.where(inside, shift_load(ext, ahead * 128 + lead, row, count), 0.0)
        at = pl.ds(row, count)
        fresh = adam(grad, states[0, at, :], states[1, at, :], states[2, at, :])
        for i in range(3):
            made[i, at, :] = jnp.where(inside, fresh[i], 0.0)

    def out(i, first, count):
        at = pl.ds(first, count)
        target = results[i].reshape(slots, 128).at[at]
        return pltpu.make_async_copy(made.at[i, at], target, out_sem.at[i, first // PART])

    parts = [(first, min(PART, slots - first)) for first in range(0, slots, PART)]
    for first, count in parts:
        whole = count // 32

        def some(k, _):
            run(pl.multiple_of(first + k * 32, 8), 32)
            return 0

        lax.fori_loop(0, whole, some, 0)
        if count % 32:
            run(first + whole * 32, count % 32)
        for i in range(3):
            out(i, first, count).start()

    head_rows = heads.shape[1]
    grad = shift_load(ext, (ahead + even) * 128 + tail, 0, head_rows)
    head_made[pl.ds(0, 32), :] = jnp.zeros((32, 128), jnp.float32)
    head_made[pl.ds(32, head_rows), :] = adam(grad, heads[0], heads[1], heads[2])[0]

    def lay(row, count):
        return shift_load(made.at[0], -lead, row, count)

    def some_rows(k, _):
        row = pl.multiple_of(k * 32, 8)
        flat[pl.ds(row, 32), :] = lay(row, 32)
        return 0

    lax.fori_loop(0, even // 32 - 1, some_rows, 0)
    index = lax.broadcasted_iota(jnp.int32, (32, 128), 0) * 128 + lax.broadcasted_iota(
        jnp.int32, (32, 128), 1
    )
    flat[pl.ds(even - 32, 32), :] = jnp.where(
        index < 32 * 128 + tail, lay(even - 32, 32), shift_load(head_made, -tail, 0, 32)
    )
    for g in range(lines):
        weight_ref[:, pl.ds(g * 128, 128)] = flat[pl.ds(g, rows, lines), :].astype(jnp.bfloat16)
    for first, count in parts:
        for i in range(3):
            out(i, first, count).wait()


PART = 256


def bucket_step(places, row_block, below, heads, master, moment_one, moment_two):
    rows, width = row_block.shape
    slots = master.shape[2] // 128
    f32 = jnp.float32
    inside = pl.BlockSpec(memory_space=pltpu.VMEM)
    anywhere = pl.BlockSpec(memory_space=pl.ANY)
    lines = width // 128
    total = -(-(9 + 8 * lines + slots + 32) // 8) * 8
    made_rows = -(-(slots + 10) // 8) * 8
    return pl.pallas_call(
        step_kernel,
        out_shape=[jax.ShapeDtypeStruct(master.shape, f32)] * 3
        + [jax.ShapeDtypeStruct((rows, width), jnp.bfloat16)],
        in_specs=[pl.BlockSpec(memory_space=pltpu.SMEM)] + [anywhere] * 6,
        out_specs=[anywhere] * 3 + [inside],
        scratch_shapes=[
            pltpu.VMEM((total, 128), f32),
            pltpu.VMEM((3, slots, 128), f32),
            pltpu.VMEM((3, made_rows, 128), f32),
            pltpu.VMEM((rows * lines, 128), f32),
            pltpu.VMEM((72, 128), f32),
            pltpu.VMEM(row_block.shape, f32),
            pltpu.VMEM(below.shape, f32),
            pltpu.VMEM((3, heads.shape[2] // 128, 128), f32),
            pltpu.SemaphoreType.DMA((8,)),
            pltpu.SemaphoreType.DMA((3, -(-slots // PART))),
        ],
        compiler_params=pltpu.CompilerParams(vmem_limit_bytes=60 * 2**20),
    )(places, row_block, below, heads, master, moment_one, moment_two)


def shards(
    tokens,
    out_grad,
    gate_up,
    route_weight,
    routes,
    down_weight,
    master,
    moment_one,
    moment_two,
    offsets,
):
    token_count, model_width = tokens.shape
    choice_count = routes.shape[1]
    hidden = gate_up.shape[2] // 2
    local_experts = master.shape[0]
    bucket_cap = master.shape[2]
    groups = lax.axis_size("expert")
    dp_count = lax.axis_size("dp")
    experts = groups * local_experts
    n = dp_count // 2
    row_count = token_count * choice_count
    capacity = 2 * row_count // experts
    flat_size = model_width * 2 * hidden
    even_size = flat_size // dp_count
    margin_size = bucket_cap - even_size
    states = (master, moment_one, moment_two)
    row_block, below_rows, router_row, heads = weight_gradient(
        tokens,
        out_grad,
        gate_up.reshape(row_count, 2 * hidden),
        route_weight,
        routes,
        down_weight[0],
        states,
        margin_size,
        n,
        experts,
        capacity,
    )
    position = lax.axis_index("dp")
    places = lax.dynamic_slice(offsets, (position,), (2,)) - even_size * (
        position + jnp.arange(2, dtype=jnp.int32)
    )
    fresh = bucket_step(places, row_block, below_rows, heads, *states)
    return (
        *fresh[:3],
        fresh[3].reshape(1, model_width // dp_count, 2 * hidden),
        router_row.reshape(token_count, choice_count),
    )


def solution(mesh):
    placed = (
        P(("dp", "expert"), None),
        P(("dp", "expert"), None),
        P(("dp", "expert"), None, None),
        P(("dp", "expert"), None),
        P(("dp", "expert"), None),
        P("expert", "dp", None),
        P("expert", "dp", None),
        P("expert", "dp", None),
        P("expert", "dp", None),
        P(),
    )
    return jax.shard_map(
        shards,
        mesh=mesh,
        in_specs=placed,
        out_specs=(
            P("expert", "dp", None),
            P("expert", "dp", None),
            P("expert", "dp", None),
            P("expert", "dp", None),
            P(("dp", "expert"), None),
        ),
        check_vma=False,
    )
```

```python
import functools

import jax
import jax.numpy as jnp
from jax import lax
from jax.experimental import pallas as pl
from jax.experimental.pallas import tpu as pltpu
from jax.sharding import PartitionSpec as P

beta_one = 0.9
beta_two = 0.95
learn_rate = 0.001
decay_rate = 0.1
adam_eps = 1e-08
adam_step = 20.0

MESH = pl.DeviceIdType.MESH


ONE_CUTS = 3
TWO_CUTS = 4


def distance(i, side):
    dx, dy = i // side, i % side
    return min(dx, 4 - dx) + min(dy, side - dy), -min(dx, 4 - dx), -min(i, 16 - i)


def groups_needed(t, span):
    most = 0
    for w in range(span):
        delta = 3 - 2 * ((2 * w) // span)
        order = [0, delta, 4 - delta, 2]
        most = max(most, *(order.index((w + way * t) // span % 4) for way in (-1, 1)))
    return most + 1


def grad_kernel(
    n,
    experts,
    tok_ref,
    grad_ref,
    saved_ref,
    weight_ref,
    route_ref,
    down_ref,
    master_ref,
    one_ref,
    two_ref,
    out_ref,
    tail_ref,
    router_ref,
    heads_ref,
    tok_in,
    grad_in,
    saved_in,
    down_in,
    pack_one,
    pack_two,
    rows_in,
    feats,
    down_wide,
    down_sib,
    down_all,
    dgu,
    score,
    score_in,
    feat_t,
    own,
    give,
    sib,
    work,
    scale,
    tail_in,
    heads_in,
    load_sem,
    one_send,
    one_recv,
    two_send,
    two_recv,
    ring_send,
    ring_recv,
    pass_send,
    pass_recv,
    twin_send,
    twin_recv,
    first_send,
    first_recv,
    score_send,
    score_recv,
    sib_send,
    sib_recv,
    sum_send,
    sum_recv,
    scale_send,
    scale_recv,
    tail_send,
    tail_recv,
    head_send,
    head_recv,
):
    half = n // 2
    count, depth = tok_ref.shape
    hidden = saved_ref.shape[1] // 2
    slots = rows_in.shape[0] // experts
    share = down_ref.shape[0]
    part = depth // 4
    rows, width = out_ref.shape
    cols = width // 2
    side = 4 if experts % 4 == 0 else experts
    dp = lax.axis_index("dp")
    me = lax.axis_index("expert")
    z, c = dp // 2, dp % 2
    other = (z * 2 + 1 - c, me)
    ahead = (lax.rem(z + 1, n) * 2 + c, me)
    behind = (lax.rem(z + n - 1, n) * 2 + c, me)
    ahead_twin = (lax.rem(z + 1, n) * 2 + 1 - c, me)
    behind_twin = (lax.rem(z + n - 1, n) * 2 + 1 - c, me)
    upper = (lax.rem(dp + 1, 2 * n), me)
    lower = (lax.rem(dp + 2 * n - 1, 2 * n), me)
    every = ((0, 0), (1, 1), (0, 1), (1, 0))
    span = n // TWO_CUTS
    group = depth // TWO_CUTS
    farthest = lax.rem(z + half, n)
    delta = 3 - 2 * ((2 * lax.rem(farthest, span)) // span)
    order = [lax.rem(farthest // span + turn, 4) for turn in (0, delta, 4 - delta, 2)]

    def group_at(p):
        return pl.ds(pl.multiple_of(order[p] * group, 128), group)


    def peer_at(dx, dy):
        x = lax.rem(me // side + dx + 4 * side, experts // side)
        return x * side + lax.rem(me % side + dy + 4 * side, side)

    def peer(i):
        return peer_at(i // side, i % side)

    far = sorted(range(1, experts), key=lambda i: distance(i, side), reverse=True)

    def remote(source, target, send, recv, device):
        return pltpu.make_async_remote_copy(
            src_ref=source,
            dst_ref=target,
            send_sem=send,
            recv_sem=recv,
            device_id=device,
            device_id_type=MESH,
        )

    barrier = pltpu.get_barrier_semaphore()
    for device in (other, ahead, behind, ahead_twin, behind_twin):
        pl.semaphore_signal(barrier, inc=1, device_id=device, device_id_type=MESH)

    def greet(i, _):
        pl.semaphore_signal(barrier, inc=1, device_id=(dp, peer(i)), device_id_type=MESH)
        return 0

    lax.fori_loop(1, experts, greet, 0)

    loads = [
        pltpu.make_async_copy(source, target, load_sem.at[i])
        for i, (source, target) in enumerate(
            ((down_ref, down_in), (grad_ref, grad_in), (saved_ref, saved_in), (tok_ref, tok_in))
        )
    ]
    for load in loads:
        load.start()

    first = remote(
        down_wide.at[:, pl.ds(pl.multiple_of((1 - c) * 2 * part, 128), 2 * part)],
        down_sib,
        first_send,
        first_recv,
        other,
    )

    def place(idx):
        return pl.ds(pl.multiple_of(lax.rem(idx + n, n) * 2 * share, 16), 2 * share)

    def down_copy(d, u, s):
        block = down_all.at[c, place(z - s if d == 0 else z + s), pl.ds(u * part, part)]
        return remote(
            block, block, ring_send.at[d, u, s], ring_recv.at[d, u, s], (ahead, behind)[d]
        )

    def twin_copy(d):
        s = half - 1
        block = down_all.at[c, place(z - s if d == 0 else z + s), pl.ds(d * part, part)]
        device = (ahead_twin, behind_twin)[d]
        return remote(block, block, twin_send.at[d], twin_recv.at[d], device)

    def pass_copy(r, half_at):
        block = down_all.at[half_at, place(z + r)]
        return remote(block, block, pass_send.at[r], pass_recv.at[r], other)

    route = route_ref[...]
    expert_id = lax.broadcasted_iota(jnp.int32, (experts, count), 0)
    onehot = jnp.where(route == expert_id, 1.0, 0.0)
    before = lax.broadcasted_iota(jnp.int32, (count, count), 0)
    after = lax.broadcasted_iota(jnp.int32, (count, count), 1)
    ahead_of = jnp.where(before < after, 1.0, 0.0).astype(jnp.bfloat16)
    earlier = jnp.dot(onehot.astype(jnp.bfloat16), ahead_of, preferred_element_type=jnp.float32)
    slot = jnp.sum(earlier * onehot, axis=0, keepdims=True).astype(jnp.int32)
    target = route * slots + slot
    slot_id = lax.broadcasted_iota(jnp.int32, (experts * slots, count), 0)
    chosen = jnp.where(slot_id == target, 1.0, 0.0)
    select = chosen.astype(jnp.bfloat16)
    slot_weight = jnp.sum(chosen * weight_ref[...].astype(jnp.float32), axis=1, keepdims=True)

    def pack(into, cuts, p, sources):
        size = into.shape[1] // cuts
        left = 0
        for source in sources:
            low, high = max(p * size, left), min((p + 1) * size, left + source.shape[1])
            if low < high:
                into[:, pl.ds(low, high - low)] = jnp.dot(
                    select,
                    source[:, pl.ds(low - left, high - low)],
                    preferred_element_type=jnp.float32,
                ).astype(jnp.bfloat16)
            left += source.shape[1]

    def block(e):
        return pl.ds(pl.multiple_of(e * slots, 16), slots)

    def one_copy(i, p):
        size = pack_one.shape[1] // ONE_CUTS
        at = pl.ds(pl.multiple_of(p * size, 128), size)
        return remote(
            pack_one.at[block(peer(i)), at],
            rows_in.at[block(me), at],
            one_send.at[i, p],
            one_recv.at[i, p],
            (dp, peer(i)),
        )

    def two_copy(i, p):
        at = group_at(p)
        return remote(
            pack_two.at[block(peer(i)), at],
            feats.at[block(me), at],
            two_send.at[i, p],
            two_recv.at[i, p],
            (dp, peer(i)),
        )

    def head_copy(i):
        source = (master_ref, one_ref, two_ref)[i]
        return remote(
            source.at[0, :, pl.ds(0, heads_in.shape[2])],
            heads_in.at[i],
            head_send.at[i],
            head_recv.at[i],
            lower,
        )

    loads[0].wait()
    down_wide[...] = down_in[...].astype(jnp.float32)
    pl.semaphore_wait(barrier, experts + 4)
    first.start()
    pack_one[:, pl.ds(depth + 2 * hidden, 128)] = jnp.broadcast_to(
        slot_weight, (experts * slots, 128)
    ).astype(jnp.bfloat16)
    def share_first():
        first.wait()
        mine = down_wide[:, pl.ds(pl.multiple_of(c * 2 * part, 128), 2 * part)]
        theirs = down_sib[...]
        top, low = jnp.where(c == 0, mine, theirs), jnp.where(c == 0, theirs, mine)
        down_all[c, place(z), :] = jnp.concatenate([top, low], axis=0).astype(jnp.bfloat16)
        for d, u in every:
            down_copy(d, u, 0).start()
        pass_copy(0, c).start()

    def forward(s):
        if s >= half:
            return
        for d, u in every:
            down_copy(d, u, s - 1).wait_recv()
            if d == u or s < half - 1:
                down_copy(d, u, s).start()
            if d == u and s == half - 1:
                twin_copy(d).start()
        pass_copy(n - s, c).start()
        pass_copy(s, c).start()

    loads[1].wait()
    loads[2].wait()
    for p in range(ONE_CUTS):
        pack(pack_one, ONE_CUTS, p, (grad_in, saved_in))
        if p == 0:
            share_first()
        for i in far:
            one_copy(i, p).start()
        forward(p + 1)
    loads[3].wait()
    for p in range(TWO_CUTS):
        pack_two[:, group_at(p)] = jnp.dot(
            select, tok_in[:, group_at(p)], preferred_element_type=jnp.float32
        ).astype(jnp.bfloat16)
        for i in far:
            two_copy(i, p).start()
        forward(p + ONE_CUTS + 1)
    for i in range(3):
        head_copy(i).start()
    rows_in[block(me), :] = pack_one[block(me), :]
    feats[block(me), :] = pack_two[block(me), :]

    for s in range(ONE_CUTS + TWO_CUTS + 1, half):
        forward(s)
    for u in range(2):
        down_copy(u, u, half - 1).wait_recv()
        twin_copy(u).wait_recv()

    def land_one(i, _):
        for p in range(ONE_CUTS):
            one_copy(i, p).wait_recv()
        return 0

    lax.fori_loop(1, experts, land_one, 0)

    def land_pass(r, _):
        pass_copy(r, 1 - c).wait_recv()
        return 0

    lax.fori_loop(0, half, land_pass, 0)
    lax.fori_loop(half + 1, n, land_pass, 0)

    tile = 256
    weight = rows_in[:, pl.ds(depth + 2 * hidden, 128)].astype(jnp.float32)[:, :1]
    total = jnp.zeros((experts * slots, 1), jnp.float32)
    for j in range(hidden // tile):
        back = sum(
            lax.dot_general(
                rows_in[:, pl.ds(h * 2 * part, 2 * part)],
                down_all[h, pl.ds(j * tile, tile), :],
                (((1,), (1,)), ((), ())),
                preferred_element_type=jnp.float32,
            )
            for h in range(2)
        )
        gate = rows_in[:, pl.ds(depth + j * tile, tile)].astype(jnp.float32)
        up = rows_in[:, pl.ds(depth + hidden + j * tile, tile)].astype(jnp.float32)
        sig = 1.0 / (1.0 + jnp.exp(-gate))
        silu = gate * sig
        total = total + jnp.sum(silu * up * back, axis=1, keepdims=True)
        scaled = weight * back
        dgu[:, pl.ds(j * tile, tile)] = (
            scaled * up * sig * (1.0 + gate * (1.0 - sig))
        ).astype(jnp.bfloat16)
        dgu[:, pl.ds(hidden + j * tile, tile)] = (scaled * silu).astype(jnp.bfloat16)
    score[...] = jnp.broadcast_to(total, score.shape)

    def score_copy(i):
        return remote(
            score.at[pl.ds(pl.multiple_of(peer(i) * slots, 8), slots)],
            score_in.at[pl.ds(pl.multiple_of(me * slots, 8), slots)],
            score_send.at[i],
            score_recv.at[i],
            (dp, peer(i)),
        )

    def land_two(p):
        def land(i, _):
            two_copy(i, p).wait_recv()
            return 0

        lax.fori_loop(1, experts, land, 0)
        at = group_at(p)
        feat_t[at, :] = feats[:, at].T

    def sib_copy(r):
        return remote(give.at[r], sib.at[r], sib_send.at[r], sib_recv.at[r], other)

    def ring_copy(d, u, s):
        return [
            remote(
                buffer.at[d, u, s],
                buffer.at[d, u, s + 1],
                send.at[d, u, s],
                recv.at[d, u, s],
                (ahead, behind)[d],
            )
            for buffer, send, recv in (
                (work, sum_send, sum_recv),
                (scale, scale_send, scale_recv),
            )
        ]

    def produce(places):
        pieces = []
        for r in places:
            owner = lax.rem(z + r, n)
            for core in (c, 1 - c):
                start = pl.multiple_of((owner * 2 + core) * rows, 16)
                pieces.append(feat_t[pl.ds(start, rows), :])
        lhs = jnp.concatenate(pieces, axis=0)
        for j in range(width // 256):
            at = pl.ds(j * 256, 256)
            prod = jnp.dot(lhs, dgu[:, at], preferred_element_type=jnp.float32)
            prod = prod.astype(jnp.bfloat16)
            for i, r in enumerate(places):
                own[r, :, at] = prod[2 * i * rows : (2 * i + 1) * rows]
                give[r, :, at] = prod[(2 * i + 1) * rows : (2 * i + 2) * rows]

    def chip_sum(r, u):
        at = pl.ds(u * cols, cols)
        return own[r, :, at].astype(jnp.float32) + sib[r, :, at].astype(jnp.float32)

    def decoded(d, u, s):
        return work[d, u, s].astype(jnp.int32).astype(jnp.float32) * scale[d, u, s]

    def step(s, streams, fresh):
        k = half - s
        for d, u in streams:
            r = k if d == 0 else n - k
            value = chip_sum(r, u)
            if (d, u) not in fresh:
                for copy in ring_copy(d, u, s - 1):
                    copy.wait_recv()
                value = value + decoded(d, u, s)
            most = jnp.maximum(jnp.max(jnp.abs(value), axis=0, keepdims=True), 1e-30)
            scale[d, u, s] = most * (1.0 / 32767.0)
            coded = jnp.round(value * (32767.0 / most))
            work[d, u, s] = coded.astype(jnp.int32).astype(jnp.int16)
            for copy in ring_copy(d, u, s):
                copy.start()

    groups = [groups_needed(t, span) for t in range(half + 1)]
    for p in range(groups[0]):
        land_two(p)
    produce([half])
    sib_copy(half).start()
    for p in range(groups[0], groups[1]):
        land_two(p)
    produce([half - 1, half + 1])
    sib_copy(half - 1).start()
    sib_copy(half + 1).start()
    sib_copy(half).wait_recv()
    step(0, every[:2], every[:2])

    def send_score(i, _):
        score_copy(i).start()
        return 0

    lax.fori_loop(1, experts, send_score, 0)
    mine_at = pl.ds(pl.multiple_of(me * slots, 8), slots)
    score_in[mine_at, :] = score[mine_at, :]

    def body(s, _):
        k = half - s
        sib_copy(k).wait_recv()
        sib_copy(n - k).wait_recv()

        @pl.when(s == 1)
        def _():
            step(s, every, every[2:])

        @pl.when(s > 1)
        def _():
            step(s, every, ())

        for p in range(groups[1], TWO_CUTS):

            @pl.when(s + 1 == min(t for t in range(half + 1) if groups[t] > p))
            def _():
                land_two(p)

        @pl.when(k > 1)
        def _():
            produce([k - 1, n - k + 1])
            sib_copy(k - 1).start()
            sib_copy(n - k + 1).start()

        return 0

    lax.fori_loop(1, half, body, 0)
    produce([0])
    sib_copy(0).start()

    def land_score(i, _):
        score_copy(i).wait()
        return 0

    lax.fori_loop(1, experts, land_score, 0)
    router_ref[...] = jnp.sum(chosen * score_in[...], axis=0, keepdims=True)

    def drain_one(i, _):
        for p in range(ONE_CUTS):
            one_copy(i, p).wait_send()
        for p in range(TWO_CUTS):
            two_copy(i, p).wait_send()
        return 0

    lax.fori_loop(1, experts, drain_one, 0)
    for i in range(3):
        head_copy(i).wait()
    heads_ref[...] = heads_in[...]

    def drain_pass(r, _):
        pass_copy(r, c).wait_send()
        return 0

    lax.fori_loop(0, half, drain_pass, 0)
    lax.fori_loop(half + 1, n, drain_pass, 0)

    def drain_down(s, _):
        for d, u in every:
            down_copy(d, u, s).wait_send()
        return 0

    lax.fori_loop(0, half - 1, drain_down, 0)
    for u in range(2):
        down_copy(u, u, half - 1).wait_send()
        twin_copy(u).wait_send()

    def drain_sum(s, _):
        for d, u in every:
            for copy in ring_copy(d, u, s):
                copy.wait_send()
        return 0

    for d, u in every[:2]:
        for copy in ring_copy(d, u, 0):
            copy.wait_send()
    lax.fori_loop(1, half - 1, drain_sum, 0)
    sib_copy(0).wait_recv()
    for u in range(2):
        for d in range(2):
            for copy in ring_copy(d, u, half - 1):
                copy.wait_recv()
        out_ref[:, pl.ds(u * cols, cols)] = chip_sum(0, u) + (
            decoded(0, u, half) + decoded(1, u, half)
        )
    last = remote(out_ref.at[pl.ds(rows - 8, 8)], tail_in, tail_send, tail_recv, upper)
    last.start()

    def drain_sib(r, _):
        sib_copy(r).wait_send()
        return 0

    lax.fori_loop(0, n, drain_sib, 0)
    drain_sum(half - 1, 0)
    last.wait()
    tail_ref[...] = tail_in[...]


def weight_gradient(
    tokens, out_grad, saved, weight, routes, down, states, margin, n, experts, slots
):
    count, depth = tokens.shape
    hidden = saved.shape[1] // 2
    width = 2 * hidden
    total = experts * slots
    rows = depth // (2 * n)
    half = n // 2
    wide = depth + width + 128
    dma = pltpu.SemaphoreType.DMA
    bf16, f32 = jnp.bfloat16, jnp.float32
    anywhere = pl.BlockSpec(memory_space=pl.ANY)
    inside = pl.BlockSpec(memory_space=pltpu.VMEM)
    return pl.pallas_call(
        functools.partial(grad_kernel, n, experts),
        out_shape=(
            jax.ShapeDtypeStruct((rows, width), f32),
            jax.ShapeDtypeStruct((8, width), f32),
            jax.ShapeDtypeStruct((1, count), f32),
            jax.ShapeDtypeStruct((3, 1, margin), f32),
        ),
        in_specs=[anywhere, anywhere, anywhere, inside, inside] + [anywhere] * 4,
        out_specs=[inside] * 4,
        scratch_shapes=[
            pltpu.VMEM(tokens.shape, bf16),
            pltpu.VMEM(out_grad.shape, bf16),
            pltpu.VMEM(saved.shape, bf16),
            pltpu.VMEM(down.shape, bf16),
            pltpu.VMEM((total, wide), bf16),
            pltpu.VMEM((total, depth), bf16),
            pltpu.VMEM((total, wide), bf16),
            pltpu.VMEM((total, depth), bf16),
            pltpu.VMEM(down.shape, f32),
            pltpu.VMEM((down.shape[0], depth // 2), f32),
            pltpu.VMEM((2, hidden, depth // 2), bf16),
            pltpu.VMEM((total, width), bf16),
            pltpu.VMEM((total, count), f32),
            pltpu.VMEM((total, count), f32),
            pltpu.VMEM((depth, total), bf16),
            pltpu.VMEM((n, rows, width), bf16),
            pltpu.VMEM((n, rows, width), bf16),
            pltpu.VMEM((n, rows, width), bf16),
            pltpu.VMEM((2, 2, half + 1, rows, width // 2), jnp.int16),
            pltpu.VMEM((2, 2, half + 1, 1, width // 2), f32),
            pltpu.VMEM((8, width), f32),
            pltpu.VMEM((3, 1, margin), f32),
            dma((4,)),
            dma((experts, ONE_CUTS)),
            dma((experts, ONE_CUTS)),
            dma((experts, TWO_CUTS)),
            dma((experts, TWO_CUTS)),
            dma((2, 2, half)),
            dma((2, 2, half)),
            dma((n,)),
            dma((n,)),
            dma((2,)),
            dma((2,)),
            dma,
            dma,
            dma((experts,)),
            dma((experts,)),
            dma((n,)),
            dma((n,)),
            dma((2, 2, half)),
            dma((2, 2, half)),
            dma((2, 2, half)),
            dma((2, 2, half)),
            dma,
            dma,
            dma((3,)),
            dma((3,)),
        ],
        compiler_params=pltpu.CompilerParams(
            collective_id=0, has_side_effects=True, vmem_limit_bytes=60 * 2**20
        ),
        cost_estimate=pl.CostEstimate(
            flops=2 * total * (depth * hidden + depth * width + count * wide),
            bytes_accessed=2 * count * wide,
            transcendentals=total * hidden,
        ),
    )(
        tokens,
        out_grad,
        saved,
        weight.reshape(1, count),
        routes.reshape(1, count),
        down,
        *states,
    )


def shift_load(ref, offset, row, count):
    start, lead = offset // 128 + row, lax.rem(offset, 128)
    lane = lax.broadcasted_iota(jnp.int32, (count, 128), 1)
    turn = lax.rem(128 - lead, 128)
    this = pltpu.roll(ref[pl.ds(start, count), :], turn, 1)
    following = pltpu.roll(ref[pl.ds(start + 1, count), :], turn, 1)
    return jnp.where(lane < 128 - lead, this, following)


def adam(grad, master, moment_one, moment_two):
    moment_new = beta_one * moment_one + (1.0 - beta_one) * grad
    square_new = beta_two * moment_two + (1.0 - beta_two) * grad * grad
    update = (moment_new * (1.0 / (1.0 - beta_one**adam_step))) / (
        jnp.sqrt(square_new * (1.0 / (1.0 - beta_two**adam_step))) + adam_eps
    )
    return master - learn_rate * (update + decay_rate * master), moment_new, square_new


def step_kernel(
    offset_ref,
    block_ref,
    below_ref,
    heads_ref,
    master_ref,
    one_ref,
    two_ref,
    router_ref,
    new_master_ref,
    new_one_ref,
    new_two_ref,
    weight_ref,
    new_router_ref,
    ext,
    states,
    made,
    flat,
    head_made,
    block,
    below,
    heads,
    in_sem,
    out_sem,
):
    rows, width = block_ref.shape
    lines = width // 128
    even = rows * lines
    position = lax.axis_index("dp")
    lead = offset_ref[position] - position * (even * 128)
    tail = offset_ref[position + 1] - (position + 1) * (even * 128)
    slots = master_ref.shape[2] // 128
    extra = slots - even
    ahead = 8 * lines
    sources = (master_ref, one_ref, two_ref)
    results = (new_master_ref, new_one_ref, new_two_ref)
    pairs = [(block_ref, block), (below_ref, below), (router_ref, new_router_ref)]
    for i in range(3):
        pairs.append((sources[i].reshape(slots, 128), states.at[i]))
        pairs.append((heads_ref.at[i].reshape(heads.shape[1], 128), heads.at[i]))
    loads = [pltpu.make_async_copy(*pair, in_sem.at[i]) for i, pair in enumerate(pairs)]
    for load in loads:
        load.start()
    for load in loads[:2]:
        load.wait()
    for g in range(lines):
        at = pl.ds(g * 128, 128)
        ext[pl.ds(g, 8, lines), :] = below[:, at]
        ext[pl.ds(ahead + g, rows, lines), :] = block[:, at]
    after = ahead + even
    ext[pl.ds(after, ext.shape[0] - after), :] = jnp.zeros((ext.shape[0] - after, 128), jnp.float32)
    held = even * 128 + tail - lead
    for load in loads[2:]:
        load.wait()

    def run(row, count):
        index = (
            (row + lax.broadcasted_iota(jnp.int32, (count, 128), 0)) * 128
            + lax.broadcasted_iota(jnp.int32, (count, 128), 1)
        )
        inside = index < held
        grad = jnp.where(inside, shift_load(ext, ahead * 128 + lead, row, count), 0.0)
        at = pl.ds(row, count)
        fresh = adam(grad, states[0, at, :], states[1, at, :], states[2, at, :])
        for i in range(3):
            made[i, at, :] = jnp.where(inside, fresh[i], 0.0)

    def out(i, first, count):
        at = pl.ds(first, count)
        target = results[i].reshape(slots, 128).at[at]
        return pltpu.make_async_copy(made.at[i, at], target, out_sem.at[i, first // PART])

    parts = [(first, min(PART, slots - first)) for first in range(0, slots, PART)]
    for first, count in parts:
        whole = count // 32

        def some(k, _):
            run(pl.multiple_of(first + k * 32, 8), 32)
            return 0

        lax.fori_loop(0, whole, some, 0, unroll=True)
        if count % 32:
            run(first + whole * 32, count % 32)
        for i in range(3):
            out(i, first, count).start()

    head_rows = heads.shape[1]
    grad = shift_load(ext, (ahead + even) * 128 + tail, 0, head_rows)
    head_made[pl.ds(0, 32), :] = jnp.zeros((32, 128), jnp.float32)
    head_made[pl.ds(32, head_rows), :] = adam(grad, heads[0], heads[1], heads[2])[0]

    def lay(row, count):
        return shift_load(made.at[0], -lead, row, count)

    def some_rows(k, _):
        row = pl.multiple_of(k * 32, 8)
        flat[pl.ds(row, 32), :] = lay(row, 32)
        return 0

    lax.fori_loop(0, even // 32 - 1, some_rows, 0, unroll=True)
    index = lax.broadcasted_iota(jnp.int32, (32, 128), 0) * 128 + lax.broadcasted_iota(
        jnp.int32, (32, 128), 1
    )
    flat[pl.ds(even - 32, 32), :] = jnp.where(
        index < 32 * 128 + tail, lay(even - 32, 32), shift_load(head_made, -tail, 0, 32)
    )
    for g in range(lines):
        weight_ref[:, pl.ds(g * 128, 128)] = flat[pl.ds(g, rows, lines), :].astype(jnp.bfloat16)
    for first, count in parts:
        for i in range(3):
            out(i, first, count).wait()


PART = 256


def bucket_step(offsets, row_block, below, heads, master, moment_one, moment_two, router):
    rows, width = row_block.shape
    slots = master.shape[2] // 128
    f32 = jnp.float32
    inside = pl.BlockSpec(memory_space=pltpu.VMEM)
    anywhere = pl.BlockSpec(memory_space=pl.ANY)
    lines = width // 128
    total = -(-(9 + 8 * lines + slots + 32) // 8) * 8
    made_rows = -(-(slots + 10) // 8) * 8
    return pl.pallas_call(
        step_kernel,
        out_shape=[jax.ShapeDtypeStruct(master.shape, f32)] * 3
        + [
            jax.ShapeDtypeStruct((rows, width), jnp.bfloat16),
            jax.ShapeDtypeStruct(router.shape, f32),
        ],
        in_specs=[pl.BlockSpec(memory_space=pltpu.SMEM)] + [anywhere] * 7,
        out_specs=[anywhere] * 3 + [inside, anywhere],
        scratch_shapes=[
            pltpu.VMEM((total, 128), f32),
            pltpu.VMEM((3, slots, 128), f32),
            pltpu.VMEM((3, made_rows, 128), f32),
            pltpu.VMEM((rows * lines, 128), f32),
            pltpu.VMEM((72, 128), f32),
            pltpu.VMEM(row_block.shape, f32),
            pltpu.VMEM(below.shape, f32),
            pltpu.VMEM((3, heads.shape[2] // 128, 128), f32),
            pltpu.SemaphoreType.DMA((9,)),
            pltpu.SemaphoreType.DMA((3, -(-slots // PART))),
        ],
        compiler_params=pltpu.CompilerParams(vmem_limit_bytes=60 * 2**20),
    )(offsets, row_block, below, heads, master, moment_one, moment_two, router)


def shards(
    tokens,
    out_grad,
    gate_up,
    route_weight,
    routes,
    down_weight,
    master,
    moment_one,
    moment_two,
    offsets,
):
    token_count, model_width = tokens.shape
    choice_count = routes.shape[1]
    hidden = gate_up.shape[2] // 2
    local_experts = master.shape[0]
    bucket_cap = master.shape[2]
    groups = lax.axis_size("expert")
    dp_count = lax.axis_size("dp")
    experts = groups * local_experts
    n = dp_count // 2
    row_count = token_count * choice_count
    capacity = 2 * row_count // experts
    flat_size = model_width * 2 * hidden
    even_size = flat_size // dp_count
    margin_size = bucket_cap - even_size
    states = (master, moment_one, moment_two)
    row_block, below_rows, router_row, heads = weight_gradient(
        tokens,
        out_grad,
        gate_up.reshape(row_count, 2 * hidden),
        route_weight,
        routes,
        down_weight[0],
        states,
        margin_size,
        n,
        experts,
        capacity,
    )
    fresh = bucket_step(offsets, row_block, below_rows, heads, *states, router_row)
    return (
        *fresh[:3],
        fresh[3].reshape(1, model_width // dp_count, 2 * hidden),
        fresh[4].reshape(token_count, choice_count),
    )


def solution(mesh):
    placed = (
        P(("dp", "expert"), None),
        P(("dp", "expert"), None),
        P(("dp", "expert"), None, None),
        P(("dp", "expert"), None),
        P(("dp", "expert"), None),
        P("expert", "dp", None),
        P("expert", "dp", None),
        P("expert", "dp", None),
        P("expert", "dp", None),
        P(),
    )
    return jax.shard_map(
        shards,
        mesh=mesh,
        in_specs=placed,
        out_specs=(
            P("expert", "dp", None),
            P("expert", "dp", None),
            P("expert", "dp", None),
            P("expert", "dp", None),
            P(("dp", "expert"), None),
        ),
        check_vma=False,
    )
```

```python
import functools

import jax
import jax.numpy as jnp
from jax import lax
from jax.experimental import pallas as pl
from jax.experimental.pallas import tpu as pltpu
from jax.sharding import PartitionSpec as P

beta_one = 0.9
beta_two = 0.95
learn_rate = 0.001
decay_rate = 0.1
adam_eps = 1e-08
adam_step = 20.0

MESH = pl.DeviceIdType.MESH


ONE_CUTS = 3
TWO_CUTS = 4


def distance(i, side):
    dx, dy = i // side, i % side
    return min(dx, 4 - dx) + min(dy, side - dy), -min(dx, 4 - dx), -min(i, 16 - i)


def groups_needed(t, span):
    most = 0
    for w in range(span):
        delta = 3 - 2 * ((2 * w) // span)
        order = [0, delta, 4 - delta, 2]
        most = max(most, *(order.index((w + way * t) // span % 4) for way in (-1, 1)))
    return most + 1


def grad_kernel(
    n,
    experts,
    tok_ref,
    grad_ref,
    saved_ref,
    weight_ref,
    route_ref,
    down_ref,
    master_ref,
    one_ref,
    two_ref,
    out_ref,
    tail_ref,
    router_ref,
    heads_ref,
    tok_in,
    grad_in,
    saved_in,
    down_in,
    pack_one,
    pack_two,
    rows_in,
    feats,
    raw,
    raw_in,
    raw_sib,
    down_all,
    dgu,
    score,
    score_in,
    feat_t,
    own,
    give,
    sib,
    work,
    scale,
    tail_in,
    heads_in,
    load_sem,
    one_send,
    one_recv,
    two_send,
    two_recv,
    ring_send,
    ring_recv,
    pass_send,
    pass_recv,
    twin_send,
    twin_recv,
    first_send,
    first_recv,
    raw_send,
    raw_recv,
    score_send,
    score_recv,
    sib_send,
    sib_recv,
    sum_send,
    sum_recv,
    scale_send,
    scale_recv,
    rest_send,
    rest_recv,
    tail_send,
    tail_recv,
    head_send,
    head_recv,
):
    half = n // 2
    count, depth = tok_ref.shape
    hidden = saved_ref.shape[1] // 2
    slots = rows_in.shape[0] // experts
    share = down_ref.shape[0]
    part = depth // 4
    rows, width = out_ref.shape
    cols = width // 2
    side = 4 if experts % 4 == 0 else experts
    dp = lax.axis_index("dp")
    me = lax.axis_index("expert")
    z, c = dp // 2, dp % 2
    other = (z * 2 + 1 - c, me)
    ahead = (lax.rem(z + 1, n) * 2 + c, me)
    behind = (lax.rem(z + n - 1, n) * 2 + c, me)
    ahead_twin = (lax.rem(z + 1, n) * 2 + 1 - c, me)
    behind_twin = (lax.rem(z + n - 1, n) * 2 + 1 - c, me)
    upper = (lax.rem(dp + 1, 2 * n), me)
    lower = (lax.rem(dp + 2 * n - 1, 2 * n), me)
    every = ((0, 0), (1, 1), (0, 1), (1, 0))
    span = n // TWO_CUTS
    group = depth // TWO_CUTS
    farthest = lax.rem(z + half, n)
    delta = 3 - 2 * ((2 * lax.rem(farthest, span)) // span)
    order = [lax.rem(farthest // span + turn, 4) for turn in (0, delta, 4 - delta, 2)]

    def group_at(p):
        return pl.ds(pl.multiple_of(order[p] * group, 128), group)


    def peer_at(dx, dy):
        x = lax.rem(me // side + dx + 4 * side, experts // side)
        return x * side + lax.rem(me % side + dy + 4 * side, side)

    def peer(i):
        return peer_at(i // side, i % side)

    far = sorted(range(1, experts), key=lambda i: distance(i, side), reverse=True)

    def remote(source, target, send, recv, device):
        return pltpu.make_async_remote_copy(
            src_ref=source,
            dst_ref=target,
            send_sem=send,
            recv_sem=recv,
            device_id=device,
            device_id_type=MESH,
        )

    barrier = pltpu.get_barrier_semaphore()
    for device in (other, ahead, behind, ahead_twin, behind_twin):
        pl.semaphore_signal(barrier, inc=1, device_id=device, device_id_type=MESH)

    def greet(i, _):
        pl.semaphore_signal(barrier, inc=1, device_id=(dp, peer(i)), device_id_type=MESH)
        return 0

    lax.fori_loop(1, experts, greet, 0)

    loads = [
        pltpu.make_async_copy(source, target, load_sem.at[i])
        for i, (source, target) in enumerate(
            ((down_ref, down_in), (grad_ref, grad_in), (saved_ref, saved_in), (tok_ref, tok_in))
        )
    ]
    for load in loads:
        load.start()

    def half_at(h):
        return pl.ds(pl.multiple_of(h * 2 * part, 128), 2 * part)

    first = remote(raw.at[:, half_at(1 - c)], raw_sib, first_send, first_recv, other)

    def raw_copy(d, h):
        chip = lax.rem(z + (1, n - 1)[d], n)
        return remote(
            raw.at[:, half_at(h)],
            raw_in.at[d, c],
            raw_send.at[d, h],
            raw_recv.at[d, c],
            (chip * 2 + h, me),
        )

    def raw_land(d, core):
        return remote(
            raw.at[:, half_at(core)],
            raw_in.at[d, core],
            raw_send.at[d, core],
            raw_recv.at[d, core],
            (ahead, behind)[d],
        )

    def place(idx):
        return pl.ds(pl.multiple_of(lax.rem(idx + n, n) * 2 * share, 16), 2 * share)

    def down_copy(d, u, s):
        block = down_all.at[c, place(z - s if d == 0 else z + s), pl.ds(u * part, part)]
        return remote(
            block, block, ring_send.at[d, u, s], ring_recv.at[d, u, s], (ahead, behind)[d]
        )

    def twin_copy(d):
        s = half - 1
        block = down_all.at[c, place(z - s if d == 0 else z + s), pl.ds(d * part, part)]
        device = (ahead_twin, behind_twin)[d]
        return remote(block, block, twin_send.at[d], twin_recv.at[d], device)

    def pass_copy(r, half_at):
        block = down_all.at[half_at, place(z + r)]
        return remote(block, block, pass_send.at[r], pass_recv.at[r], other)

    route = route_ref[...]
    expert_id = lax.broadcasted_iota(jnp.int32, (experts, count), 0)
    onehot = jnp.where(route == expert_id, 1.0, 0.0)
    before = lax.broadcasted_iota(jnp.int32, (count, count), 0)
    after = lax.broadcasted_iota(jnp.int32, (count, count), 1)
    ahead_of = jnp.where(before < after, 1.0, 0.0).astype(jnp.bfloat16)
    earlier = jnp.dot(onehot.astype(jnp.bfloat16), ahead_of, preferred_element_type=jnp.float32)
    slot = jnp.sum(earlier * onehot, axis=0, keepdims=True).astype(jnp.int32)
    target = route * slots + slot
    slot_id = lax.broadcasted_iota(jnp.int32, (experts * slots, count), 0)
    chosen = jnp.where(slot_id == target, 1.0, 0.0)
    select = chosen.astype(jnp.bfloat16)
    slot_weight = jnp.sum(chosen * weight_ref[...].astype(jnp.float32), axis=1, keepdims=True)

    def pack(into, cuts, p, sources):
        size = into.shape[1] // cuts
        left = 0
        for source in sources:
            low, high = max(p * size, left), min((p + 1) * size, left + source.shape[1])
            if low < high:
                into[:, pl.ds(low, high - low)] = jnp.dot(
                    select,
                    source[:, pl.ds(low - left, high - low)],
                    preferred_element_type=jnp.float32,
                ).astype(jnp.bfloat16)
            left += source.shape[1]

    def block(e):
        return pl.ds(pl.multiple_of(e * slots, 16), slots)

    def one_copy(i, p):
        size = pack_one.shape[1] // ONE_CUTS
        at = pl.ds(pl.multiple_of(p * size, 128), size)
        return remote(
            pack_one.at[block(peer(i)), at],
            rows_in.at[block(me), at],
            one_send.at[i, p],
            one_recv.at[i, p],
            (dp, peer(i)),
        )

    def two_copy(i, p):
        at = group_at(p)
        return remote(
            pack_two.at[block(peer(i)), at],
            feats.at[block(me), at],
            two_send.at[i, p],
            two_recv.at[i, p],
            (dp, peer(i)),
        )

    def head_copy(i):
        source = (master_ref, one_ref, two_ref)[i]
        return remote(
            source.at[0, :, pl.ds(0, heads_in.shape[2])],
            heads_in.at[i],
            head_send.at[i],
            head_recv.at[i],
            lower,
        )

    loads[0].wait()
    shard = down_in[...].astype(jnp.float32)
    if raw.shape[0] > share:
        spare = jnp.zeros((raw.shape[0] - share, depth), jnp.float32)
        shard = jnp.concatenate([shard, spare], axis=0)
    raw[...] = shard.astype(jnp.bfloat16)
    pl.semaphore_wait(barrier, experts + 4)
    for h in range(2):
        for d in range(2):
            raw_copy(d, h).start()
    first.start()
    pack_one[:, pl.ds(depth + 2 * hidden, 128)] = jnp.broadcast_to(
        slot_weight, (experts * slots, 128)
    ).astype(jnp.bfloat16)
    def joined(top, low):
        pieces = [top.astype(jnp.float32)[:share], low.astype(jnp.float32)[:share]]
        return jnp.concatenate(pieces, axis=0).astype(jnp.bfloat16)

    def share_first():
        first.wait()
        mine = raw[:, half_at(c)].astype(jnp.float32)
        theirs = raw_sib[...].astype(jnp.float32)
        down_all[c, place(z), :] = joined(
            jnp.where(c == 0, mine, theirs), jnp.where(c == 0, theirs, mine)
        )
        pass_copy(0, c).start()

    def forward(s):
        if s >= half:
            return
        if s == 1:
            for d in range(2):
                raw_land(d, 0).wait_recv()
                raw_land(d, 1).wait_recv()
                block_at = place(z - 1 if d == 0 else z + 1)
                down_all[c, block_at, :] = joined(raw_in[d, 0], raw_in[d, 1])
        for d, u in every:
            if s > 1:
                down_copy(d, u, s - 1).wait_recv()
            if d == u or s < half - 1:
                down_copy(d, u, s).start()
            if d == u and s == half - 1:
                twin_copy(d).start()
        pass_copy(n - s, c).start()
        pass_copy(s, c).start()

    loads[1].wait()
    loads[2].wait()
    for p in range(ONE_CUTS):
        pack(pack_one, ONE_CUTS, p, (grad_in, saved_in))
        if p == 0:
            share_first()
        for i in far:
            one_copy(i, p).start()
        forward(p + 1)
    loads[3].wait()
    for p in range(TWO_CUTS):
        pack_two[:, group_at(p)] = jnp.dot(
            select, tok_in[:, group_at(p)], preferred_element_type=jnp.float32
        ).astype(jnp.bfloat16)
        for i in far:
            two_copy(i, p).start()
        forward(p + ONE_CUTS + 1)
    for i in range(3):
        head_copy(i).start()
    rows_in[block(me), :] = pack_one[block(me), :]
    feats[block(me), :] = pack_two[block(me), :]

    for s in range(ONE_CUTS + TWO_CUTS + 1, half):
        forward(s)
    for u in range(2):
        down_copy(u, u, half - 1).wait_recv()
        twin_copy(u).wait_recv()

    def land_one(i, _):
        for p in range(ONE_CUTS):
            one_copy(i, p).wait_recv()
        return 0

    lax.fori_loop(1, experts, land_one, 0)

    def land_pass(r, _):
        pass_copy(r, 1 - c).wait_recv()
        return 0

    lax.fori_loop(0, half, land_pass, 0)
    lax.fori_loop(half + 1, n, land_pass, 0)

    tile = 256
    weight = rows_in[:, pl.ds(depth + 2 * hidden, 128)].astype(jnp.float32)[:, :1]
    total = jnp.zeros((experts * slots, 1), jnp.float32)
    for j in range(hidden // tile):
        back = sum(
            lax.dot_general(
                rows_in[:, pl.ds(h * 2 * part, 2 * part)],
                down_all[h, pl.ds(j * tile, tile), :],
                (((1,), (1,)), ((), ())),
                preferred_element_type=jnp.float32,
            )
            for h in range(2)
        )
        gate = rows_in[:, pl.ds(depth + j * tile, tile)].astype(jnp.float32)
        up = rows_in[:, pl.ds(depth + hidden + j * tile, tile)].astype(jnp.float32)
        sig = 1.0 / (1.0 + jnp.exp(-gate))
        silu = gate * sig
        total = total + jnp.sum(silu * up * back, axis=1, keepdims=True)
        scaled = weight * back
        dgu[:, pl.ds(j * tile, tile)] = (
            scaled * up * sig * (1.0 + gate * (1.0 - sig))
        ).astype(jnp.bfloat16)
        dgu[:, pl.ds(hidden + j * tile, tile)] = (scaled * silu).astype(jnp.bfloat16)
    score[...] = jnp.broadcast_to(total, score.shape)

    def score_copy(i):
        return remote(
            score.at[pl.ds(pl.multiple_of(peer(i) * slots, 8), slots)],
            score_in.at[pl.ds(pl.multiple_of(me * slots, 8), slots)],
            score_send.at[i],
            score_recv.at[i],
            (dp, peer(i)),
        )

    def land_two(p):
        def land(i, _):
            two_copy(i, p).wait_recv()
            return 0

        lax.fori_loop(1, experts, land, 0)
        at = group_at(p)
        feat_t[at, :] = feats[:, at].T

    def sib_copy(r):
        return remote(give.at[r], sib.at[r], sib_send.at[r], sib_recv.at[r], other)

    def ring_copy(d, u, s):
        return [
            remote(
                buffer.at[d, u, s],
                buffer.at[d, u, s + 1],
                send.at[d, u, s],
                recv.at[d, u, s],
                (ahead, behind)[d],
            )
            for buffer, send, recv in (
                (work, sum_send, sum_recv),
                (scale, scale_send, scale_recv),
            )
        ]

    late, early = pl.ds(rows - 16, 16), pl.ds(0, rows - 16)

    def last_copy(d, u, pieces=(0, 1, 2)):
        s = half - 1
        parts = (
            (scale.at[d, u, s], scale.at[d, u, s + 1], scale_send, scale_recv),
            (work.at[d, u, s, late], work.at[d, u, s + 1, late], sum_send, sum_recv),
            (work.at[d, u, s, early], work.at[d, u, s + 1, early], rest_send, rest_recv),
        )
        copies = []
        for i in pieces:
            source, target, send, recv = parts[i]
            slot = (d, u) if i == 2 else (d, u, s)
            copies.append(
                remote(source, target, send.at[slot], recv.at[slot], (ahead, behind)[d])
            )
        return copies

    def produce(places):
        pieces = []
        for r in places:
            owner = lax.rem(z + r, n)
            for core in (c, 1 - c):
                start = pl.multiple_of((owner * 2 + core) * rows, 16)
                pieces.append(feat_t[pl.ds(start, rows), :])
        lhs = jnp.concatenate(pieces, axis=0)
        for j in range(width // 256):
            at = pl.ds(j * 256, 256)
            prod = jnp.dot(lhs, dgu[:, at], preferred_element_type=jnp.float32)
            prod = prod.astype(jnp.bfloat16)
            for i, r in enumerate(places):
                own[r, :, at] = prod[2 * i * rows : (2 * i + 1) * rows]
                give[r, :, at] = prod[(2 * i + 1) * rows : (2 * i + 2) * rows]

    def chip_sum(r, u, at=pl.ds(0, rows)):
        across = pl.ds(u * cols, cols)
        return own[r, at, across].astype(jnp.float32) + sib[r, at, across].astype(jnp.float32)

    def decoded(d, u, s, at=pl.ds(0, rows)):
        return work[d, u, s, at, :].astype(jnp.int32).astype(jnp.float32) * scale[d, u, s]

    def step(s, streams, fresh, last=False):
        k = half - s
        for d, u in streams:
            r = k if d == 0 else n - k
            value = chip_sum(r, u)
            if (d, u) not in fresh:
                for copy in ring_copy(d, u, s - 1):
                    copy.wait_recv()
                value = value + decoded(d, u, s)
            most = jnp.maximum(jnp.max(jnp.abs(value), axis=0, keepdims=True), 1e-30)
            scale[d, u, s] = most * (1.0 / 32767.0)
            coded = jnp.round(value * (32767.0 / most))
            work[d, u, s] = coded.astype(jnp.int32).astype(jnp.int16)
            for copy in last_copy(d, u) if last else ring_copy(d, u, s):
                copy.start()

    groups = [groups_needed(t, span) for t in range(half + 1)]
    needed = [min(t for t in range(half + 1) if groups[t] > p) for p in range(TWO_CUTS)]

    def prepare(t):
        for p in range(TWO_CUTS):
            if needed[p] == t:
                land_two(p)
        k = half - t
        places = [k] if k in (0, half) else [k, n - k]
        produce(places)
        for r in places:
            sib_copy(r).start()

    prepare(0)
    prepare(1)
    sib_copy(half).wait_recv()
    step(0, every[:2], every[:2])
    prepare(2)

    def send_score(i, _):
        score_copy(i).start()
        return 0

    lax.fori_loop(1, experts, send_score, 0)
    mine_at = pl.ds(pl.multiple_of(me * slots, 8), slots)
    score_in[mine_at, :] = score[mine_at, :]

    def body(s, _):
        k = half - s
        sib_copy(k).wait_recv()
        sib_copy(n - k).wait_recv()

        @pl.when(s == 1)
        def _():
            step(s, every, every[2:])

        @pl.when(s > 1)
        def _():
            step(s, every, ())

        for p in range(TWO_CUTS):
            if needed[p] > 2:

                @pl.when(s + 2 == needed[p])
                def _():
                    land_two(p)

        produce([k - 2, n - k + 2])
        sib_copy(k - 2).start()
        sib_copy(n - k + 2).start()
        return 0

    lax.fori_loop(1, half - 2, body, 0)
    for s in range(max(1, half - 2), half):
        k = half - s
        sib_copy(k).wait_recv()
        sib_copy(n - k).wait_recv()
        step(s, every, every[2:] if s == 1 else (), s == half - 1)
        if k == 2:
            prepare(half)

    def land_score(i, _):
        score_copy(i).wait()
        return 0

    lax.fori_loop(1, experts, land_score, 0)
    router_ref[...] = jnp.sum(chosen * score_in[...], axis=0, keepdims=True)

    def drain_one(i, _):
        for p in range(ONE_CUTS):
            one_copy(i, p).wait_send()
        for p in range(TWO_CUTS):
            two_copy(i, p).wait_send()
        return 0

    lax.fori_loop(1, experts, drain_one, 0)
    for i in range(3):
        head_copy(i).wait()
    heads_ref[...] = heads_in[...]

    def drain_pass(r, _):
        pass_copy(r, c).wait_send()
        return 0

    lax.fori_loop(0, half, drain_pass, 0)
    lax.fori_loop(half + 1, n, drain_pass, 0)

    def drain_down(s, _):
        for d, u in every:
            down_copy(d, u, s).wait_send()
        return 0

    lax.fori_loop(1, half - 1, drain_down, 0)
    for d in range(2):
        for h in range(2):
            raw_copy(d, h).wait_send()
    for u in range(2):
        down_copy(u, u, half - 1).wait_send()
        twin_copy(u).wait_send()

    def drain_sum(s, _):
        for d, u in every:
            for copy in ring_copy(d, u, s):
                copy.wait_send()
        return 0

    for d, u in every[:2]:
        for copy in ring_copy(d, u, 0):
            copy.wait_send()
    lax.fori_loop(1, half - 1, drain_sum, 0)
    sib_copy(0).wait_recv()

    def finish(at, pieces):
        for u in range(2):
            for d in range(2):
                for copy in last_copy(d, u, pieces):
                    copy.wait_recv()
            out_ref[at, pl.ds(u * cols, cols)] = chip_sum(0, u, at) + (
                decoded(0, u, half, at) + decoded(1, u, half, at)
            )

    finish(late, (0, 1))
    last = remote(out_ref.at[pl.ds(rows - 8, 8)], tail_in, tail_send, tail_recv, upper)
    last.start()
    finish(early, (2,))

    def drain_sib(r, _):
        sib_copy(r).wait_send()
        return 0

    lax.fori_loop(0, n, drain_sib, 0)
    for d, u in every:
        for copy in last_copy(d, u):
            copy.wait_send()
    last.wait()
    tail_ref[...] = tail_in[...]


def weight_gradient(
    tokens, out_grad, saved, weight, routes, down, states, margin, n, experts, slots
):
    count, depth = tokens.shape
    hidden = saved.shape[1] // 2
    width = 2 * hidden
    total = experts * slots
    rows = depth // (2 * n)
    half = n // 2
    wide = depth + width + 128
    padded = -(-down.shape[0] // 16) * 16
    dma = pltpu.SemaphoreType.DMA
    bf16, f32 = jnp.bfloat16, jnp.float32
    anywhere = pl.BlockSpec(memory_space=pl.ANY)
    inside = pl.BlockSpec(memory_space=pltpu.VMEM)
    return pl.pallas_call(
        functools.partial(grad_kernel, n, experts),
        out_shape=(
            jax.ShapeDtypeStruct((rows, width), f32),
            jax.ShapeDtypeStruct((8, width), f32),
            jax.ShapeDtypeStruct((1, count), f32),
            jax.ShapeDtypeStruct((3, 1, margin), f32),
        ),
        in_specs=[anywhere, anywhere, anywhere, inside, inside] + [anywhere] * 4,
        out_specs=[inside] * 4,
        scratch_shapes=[
            pltpu.VMEM(tokens.shape, bf16),
            pltpu.VMEM(out_grad.shape, bf16),
            pltpu.VMEM(saved.shape, bf16),
            pltpu.VMEM(down.shape, bf16),
            pltpu.VMEM((total, wide), bf16),
            pltpu.VMEM((total, depth), bf16),
            pltpu.VMEM((total, wide), bf16),
            pltpu.VMEM((total, depth), bf16),
            pltpu.VMEM((padded, depth), bf16),
            pltpu.VMEM((2, 2, padded, depth // 2), bf16),
            pltpu.VMEM((padded, depth // 2), bf16),
            pltpu.VMEM((2, hidden, depth // 2), bf16),
            pltpu.VMEM((total, width), bf16),
            pltpu.VMEM((total, count), f32),
            pltpu.VMEM((total, count), f32),
            pltpu.VMEM((depth, total), bf16),
            pltpu.VMEM((n, rows, width), bf16),
            pltpu.VMEM((n, rows, width), bf16),
            pltpu.VMEM((n, rows, width), bf16),
            pltpu.VMEM((2, 2, half + 1, rows, width // 2), jnp.int16),
            pltpu.VMEM((2, 2, half + 1, 1, width // 2), f32),
            pltpu.VMEM((8, width), f32),
            pltpu.VMEM((3, 1, margin), f32),
            dma((4,)),
            dma((experts, ONE_CUTS)),
            dma((experts, ONE_CUTS)),
            dma((experts, TWO_CUTS)),
            dma((experts, TWO_CUTS)),
            dma((2, 2, half)),
            dma((2, 2, half)),
            dma((n,)),
            dma((n,)),
            dma((2,)),
            dma((2,)),
            dma,
            dma,
            dma((2, 2)),
            dma((2, 2)),
            dma((experts,)),
            dma((experts,)),
            dma((n,)),
            dma((n,)),
            dma((2, 2, half)),
            dma((2, 2, half)),
            dma((2, 2, half)),
            dma((2, 2, half)),
            dma((2, 2)),
            dma((2, 2)),
            dma,
            dma,
            dma((3,)),
            dma((3,)),
        ],
        compiler_params=pltpu.CompilerParams(
            collective_id=0, has_side_effects=True, vmem_limit_bytes=60 * 2**20
        ),
        cost_estimate=pl.CostEstimate(
            flops=2 * total * (depth * hidden + depth * width + count * wide),
            bytes_accessed=2 * count * wide,
            transcendentals=total * hidden,
        ),
    )(
        tokens,
        out_grad,
        saved,
        weight.reshape(1, count),
        routes.reshape(1, count),
        down,
        *states,
    )


def shift_load(ref, offset, row, count):
    start, lead = offset // 128 + row, lax.rem(offset, 128)
    lane = lax.broadcasted_iota(jnp.int32, (count, 128), 1)
    turn = lax.rem(128 - lead, 128)
    this = pltpu.roll(ref[pl.ds(start, count), :], turn, 1)
    following = pltpu.roll(ref[pl.ds(start + 1, count), :], turn, 1)
    return jnp.where(lane < 128 - lead, this, following)


def adam(grad, master, moment_one, moment_two):
    moment_new = beta_one * moment_one + (1.0 - beta_one) * grad
    square_new = beta_two * moment_two + (1.0 - beta_two) * grad * grad
    update = (moment_new * (1.0 / (1.0 - beta_one**adam_step))) / (
        jnp.sqrt(square_new * (1.0 / (1.0 - beta_two**adam_step))) + adam_eps
    )
    return master - learn_rate * (update + decay_rate * master), moment_new, square_new


def step_kernel(
    offset_ref,
    block_ref,
    below_ref,
    heads_ref,
    master_ref,
    one_ref,
    two_ref,
    router_ref,
    new_master_ref,
    new_one_ref,
    new_two_ref,
    weight_ref,
    new_router_ref,
    ext,
    states,
    made,
    flat,
    head_made,
    block,
    below,
    heads,
    in_sem,
    out_sem,
):
    rows, width = block_ref.shape
    lines = width // 128
    even = rows * lines
    position = lax.axis_index("dp")
    lead = offset_ref[position] - position * (even * 128)
    tail = offset_ref[position + 1] - (position + 1) * (even * 128)
    slots = master_ref.shape[2] // 128
    extra = slots - even
    ahead = 8 * lines
    sources = (master_ref, one_ref, two_ref)
    results = (new_master_ref, new_one_ref, new_two_ref)
    pairs = [(block_ref, block), (below_ref, below), (router_ref, new_router_ref)]
    for i in range(3):
        pairs.append((sources[i].reshape(slots, 128), states.at[i]))
        pairs.append((heads_ref.at[i].reshape(heads.shape[1], 128), heads.at[i]))
    loads = [pltpu.make_async_copy(*pair, in_sem.at[i]) for i, pair in enumerate(pairs)]
    for load in loads:
        load.start()
    for load in loads[:2]:
        load.wait()
    for g in range(lines):
        at = pl.ds(g * 128, 128)
        ext[pl.ds(g, 8, lines), :] = below[:, at]
        ext[pl.ds(ahead + g, rows, lines), :] = block[:, at]
    after = ahead + even
    ext[pl.ds(after, ext.shape[0] - after), :] = jnp.zeros((ext.shape[0] - after, 128), jnp.float32)
    held = even * 128 + tail - lead
    for load in loads[2:]:
        load.wait()

    def run(row, count):
        index = (
            (row + lax.broadcasted_iota(jnp.int32, (count, 128), 0)) * 128
            + lax.broadcasted_iota(jnp.int32, (count, 128), 1)
        )
        inside = index < held
        grad = jnp.where(inside, shift_load(ext, ahead * 128 + lead, row, count), 0.0)
        at = pl.ds(row, count)
        fresh = adam(grad, states[0, at, :], states[1, at, :], states[2, at, :])
        for i in range(3):
            made[i, at, :] = jnp.where(inside, fresh[i], 0.0)

    def out(i, first, count):
        at = pl.ds(first, count)
        target = results[i].reshape(slots, 128).at[at]
        return pltpu.make_async_copy(made.at[i, at], target, out_sem.at[i, first // PART])

    parts = [(first, min(PART, slots - first)) for first in range(0, slots, PART)]
    for first, count in parts:
        whole = count // 32

        def some(k, _):
            run(pl.multiple_of(first + k * 32, 8), 32)
            return 0

        lax.fori_loop(0, whole, some, 0, unroll=True)
        if count % 32:
            run(first + whole * 32, count % 32)
        for i in range(3):
            out(i, first, count).start()

    head_rows = heads.shape[1]
    grad = shift_load(ext, (ahead + even) * 128 + tail, 0, head_rows)
    head_made[pl.ds(0, 32), :] = jnp.zeros((32, 128), jnp.float32)
    head_made[pl.ds(32, head_rows), :] = adam(grad, heads[0], heads[1], heads[2])[0]

    def lay(row, count):
        return shift_load(made.at[0], -lead, row, count)

    def some_rows(k, _):
        row = pl.multiple_of(k * 32, 8)
        flat[pl.ds(row, 32), :] = lay(row, 32)
        return 0

    lax.fori_loop(0, even // 32 - 1, some_rows, 0, unroll=True)
    index = lax.broadcasted_iota(jnp.int32, (32, 128), 0) * 128 + lax.broadcasted_iota(
        jnp.int32, (32, 128), 1
    )
    flat[pl.ds(even - 32, 32), :] = jnp.where(
        index < 32 * 128 + tail, lay(even - 32, 32), shift_load(head_made, -tail, 0, 32)
    )
    for g in range(lines):
        weight_ref[:, pl.ds(g * 128, 128)] = flat[pl.ds(g, rows, lines), :].astype(jnp.bfloat16)
    for first, count in parts:
        for i in range(3):
            out(i, first, count).wait()


PART = 256


def bucket_step(offsets, row_block, below, heads, master, moment_one, moment_two, router):
    rows, width = row_block.shape
    slots = master.shape[2] // 128
    f32 = jnp.float32
    inside = pl.BlockSpec(memory_space=pltpu.VMEM)
    anywhere = pl.BlockSpec(memory_space=pl.ANY)
    lines = width // 128
    total = -(-(9 + 8 * lines + slots + 32) // 8) * 8
    made_rows = -(-(slots + 10) // 8) * 8
    return pl.pallas_call(
        step_kernel,
        out_shape=[jax.ShapeDtypeStruct(master.shape, f32)] * 3
        + [
            jax.ShapeDtypeStruct((rows, width), jnp.bfloat16),
            jax.ShapeDtypeStruct(router.shape, f32),
        ],
        in_specs=[pl.BlockSpec(memory_space=pltpu.SMEM)] + [anywhere] * 7,
        out_specs=[anywhere] * 3 + [inside, anywhere],
        scratch_shapes=[
            pltpu.VMEM((total, 128), f32),
            pltpu.VMEM((3, slots, 128), f32),
            pltpu.VMEM((3, made_rows, 128), f32),
            pltpu.VMEM((rows * lines, 128), f32),
            pltpu.VMEM((72, 128), f32),
            pltpu.VMEM(row_block.shape, f32),
            pltpu.VMEM(below.shape, f32),
            pltpu.VMEM((3, heads.shape[2] // 128, 128), f32),
            pltpu.SemaphoreType.DMA((9,)),
            pltpu.SemaphoreType.DMA((3, -(-slots // PART))),
        ],
        compiler_params=pltpu.CompilerParams(vmem_limit_bytes=60 * 2**20),
    )(offsets, row_block, below, heads, master, moment_one, moment_two, router)


def shards(
    tokens,
    out_grad,
    gate_up,
    route_weight,
    routes,
    down_weight,
    master,
    moment_one,
    moment_two,
    offsets,
):
    token_count, model_width = tokens.shape
    choice_count = routes.shape[1]
    hidden = gate_up.shape[2] // 2
    local_experts = master.shape[0]
    bucket_cap = master.shape[2]
    groups = lax.axis_size("expert")
    dp_count = lax.axis_size("dp")
    experts = groups * local_experts
    n = dp_count // 2
    row_count = token_count * choice_count
    capacity = 2 * row_count // experts
    flat_size = model_width * 2 * hidden
    even_size = flat_size // dp_count
    margin_size = bucket_cap - even_size
    states = (master, moment_one, moment_two)
    row_block, below_rows, router_row, heads = weight_gradient(
        tokens,
        out_grad,
        gate_up.reshape(row_count, 2 * hidden),
        route_weight,
        routes,
        down_weight[0],
        states,
        margin_size,
        n,
        experts,
        capacity,
    )
    fresh = bucket_step(offsets, row_block, below_rows, heads, *states, router_row)
    return (
        *fresh[:3],
        fresh[3].reshape(1, model_width // dp_count, 2 * hidden),
        fresh[4].reshape(token_count, choice_count),
    )


def solution(mesh):
    placed = (
        P(("dp", "expert"), None),
        P(("dp", "expert"), None),
        P(("dp", "expert"), None, None),
        P(("dp", "expert"), None),
        P(("dp", "expert"), None),
        P("expert", "dp", None),
        P("expert", "dp", None),
        P("expert", "dp", None),
        P("expert", "dp", None),
        P(),
    )
    return jax.shard_map(
        shards,
        mesh=mesh,
        in_specs=placed,
        out_specs=(
            P("expert", "dp", None),
            P("expert", "dp", None),
            P("expert", "dp", None),
            P("expert", "dp", None),
            P(("dp", "expert"), None),
        ),
        check_vma=False,
    )
```

```python
import functools

import jax
import jax.numpy as jnp
from jax import lax
from jax.experimental import pallas as pl
from jax.experimental.pallas import tpu as pltpu
from jax.sharding import PartitionSpec as P

beta_one = 0.9
beta_two = 0.95
learn_rate = 0.001
decay_rate = 0.1
adam_eps = 1e-08
adam_step = 20.0

MESH = pl.DeviceIdType.MESH


ONE_CUTS = 3
TWO_CUTS = 4


def distance(i, side):
    dx, dy = i // side, i % side
    return min(dx, 4 - dx) + min(dy, side - dy), -min(dx, 4 - dx), -min(i, 16 - i)


def groups_needed(t, span):
    most = 0
    for w in range(span):
        delta = 3 - 2 * ((2 * w) // span)
        order = [0, delta, 4 - delta, 2]
        most = max(most, *(order.index((w + way * t) // span % 4) for way in (-1, 1)))
    return most + 1


def grad_kernel(
    n,
    experts,
    tok_ref,
    grad_ref,
    saved_ref,
    weight_ref,
    route_ref,
    down_ref,
    master_ref,
    one_ref,
    two_ref,
    out_ref,
    tail_ref,
    router_ref,
    heads_ref,
    tok_in,
    grad_in,
    saved_in,
    down_in,
    pack_one,
    pack_two,
    rows_in,
    feats,
    raw,
    raw_in,
    raw_sib,
    down_all,
    dgu,
    score,
    score_in,
    feat_t,
    own,
    give,
    sib,
    work,
    scale,
    tail_in,
    heads_in,
    load_sem,
    one_send,
    one_recv,
    two_send,
    two_recv,
    ring_send,
    ring_recv,
    pass_send,
    pass_recv,
    twin_send,
    twin_recv,
    first_send,
    first_recv,
    raw_send,
    raw_recv,
    score_send,
    score_recv,
    sib_send,
    sib_recv,
    sum_send,
    sum_recv,
    scale_send,
    scale_recv,
    rest_send,
    rest_recv,
    tail_send,
    tail_recv,
    head_send,
    head_recv,
):
    half = n // 2
    count, depth = tok_ref.shape
    hidden = saved_ref.shape[1] // 2
    slots = rows_in.shape[0] // experts
    share = down_ref.shape[0]
    part = depth // 4
    rows, width = out_ref.shape
    cols = width // 2
    side = 4 if experts % 4 == 0 else experts
    dp = lax.axis_index("dp")
    me = lax.axis_index("expert")
    z, c = dp // 2, dp % 2
    other = (z * 2 + 1 - c, me)
    ahead = (lax.rem(z + 1, n) * 2 + c, me)
    behind = (lax.rem(z + n - 1, n) * 2 + c, me)
    ahead_twin = (lax.rem(z + 1, n) * 2 + 1 - c, me)
    behind_twin = (lax.rem(z + n - 1, n) * 2 + 1 - c, me)
    upper = (lax.rem(dp + 1, 2 * n), me)
    lower = (lax.rem(dp + 2 * n - 1, 2 * n), me)
    every = ((0, 0), (1, 1), (0, 1), (1, 0))
    span = n // TWO_CUTS
    group = depth // TWO_CUTS
    farthest = lax.rem(z + half, n)
    delta = 3 - 2 * ((2 * lax.rem(farthest, span)) // span)
    order = [lax.rem(farthest // span + turn, 4) for turn in (0, delta, 4 - delta, 2)]

    def group_at(p):
        return pl.ds(pl.multiple_of(order[p] * group, 128), group)


    def peer_at(dx, dy):
        x = lax.rem(me // side + dx + 4 * side, experts // side)
        return x * side + lax.rem(me % side + dy + 4 * side, side)

    def peer(i):
        return peer_at(i // side, i % side)

    far = sorted(range(1, experts), key=lambda i: distance(i, side), reverse=True)

    def remote(source, target, send, recv, device):
        return pltpu.make_async_remote_copy(
            src_ref=source,
            dst_ref=target,
            send_sem=send,
            recv_sem=recv,
            device_id=device,
            device_id_type=MESH,
        )

    loads = [
        pltpu.make_async_copy(source, target, load_sem.at[i])
        for i, (source, target) in enumerate(
            ((down_ref, down_in), (grad_ref, grad_in), (saved_ref, saved_in), (tok_ref, tok_in))
        )
    ]
    for load in loads:
        load.start()

    barrier = pltpu.get_barrier_semaphore()
    for device in (other, ahead, behind, ahead_twin, behind_twin):
        pl.semaphore_signal(barrier, inc=1, device_id=device, device_id_type=MESH)

    def greet(i, _):
        pl.semaphore_signal(barrier, inc=1, device_id=(dp, peer(i)), device_id_type=MESH)
        return 0

    lax.fori_loop(1, experts, greet, 0)

    def half_at(h):
        return pl.ds(pl.multiple_of(h * 2 * part, 128), 2 * part)

    first = remote(raw.at[:, half_at(1 - c)], raw_sib, first_send, first_recv, other)

    def raw_copy(d, h):
        chip = lax.rem(z + (1, n - 1)[d], n)
        return remote(
            raw.at[:, half_at(h)],
            raw_in.at[d, c],
            raw_send.at[d, h],
            raw_recv.at[d, c],
            (chip * 2 + h, me),
        )

    def raw_land(d, core):
        return remote(
            raw.at[:, half_at(core)],
            raw_in.at[d, core],
            raw_send.at[d, core],
            raw_recv.at[d, core],
            (ahead, behind)[d],
        )

    def place(idx):
        return pl.ds(pl.multiple_of(lax.rem(idx + n, n) * 2 * share, 16), 2 * share)

    def down_copy(d, u, s):
        block = down_all.at[c, place(z - s if d == 0 else z + s), pl.ds(u * part, part)]
        return remote(
            block, block, ring_send.at[d, u, s], ring_recv.at[d, u, s], (ahead, behind)[d]
        )

    def twin_copy(d):
        s = half - 1
        block = down_all.at[c, place(z - s if d == 0 else z + s), pl.ds(d * part, part)]
        device = (ahead_twin, behind_twin)[d]
        return remote(block, block, twin_send.at[d], twin_recv.at[d], device)

    def pass_copy(r, half_at):
        block = down_all.at[half_at, place(z + r)]
        return remote(block, block, pass_send.at[r], pass_recv.at[r], other)

    route = route_ref[...]
    expert_id = lax.broadcasted_iota(jnp.int32, (experts, count), 0)
    onehot = jnp.where(route == expert_id, 1.0, 0.0)
    before = lax.broadcasted_iota(jnp.int32, (count, count), 0)
    after = lax.broadcasted_iota(jnp.int32, (count, count), 1)
    ahead_of = jnp.where(before < after, 1.0, 0.0).astype(jnp.bfloat16)
    earlier = jnp.dot(onehot.astype(jnp.bfloat16), ahead_of, preferred_element_type=jnp.float32)
    slot = jnp.sum(earlier * onehot, axis=0, keepdims=True).astype(jnp.int32)
    target = route * slots + slot
    slot_id = lax.broadcasted_iota(jnp.int32, (experts * slots, count), 0)
    chosen = jnp.where(slot_id == target, 1.0, 0.0)
    select = chosen.astype(jnp.bfloat16)
    slot_weight = jnp.sum(chosen * weight_ref[...].astype(jnp.float32), axis=1, keepdims=True)

    def pack(into, cuts, p, sources):
        size = into.shape[1] // cuts
        left = 0
        for source in sources:
            low, high = max(p * size, left), min((p + 1) * size, left + source.shape[1])
            if low < high:
                into[:, pl.ds(low, high - low)] = jnp.dot(
                    select,
                    source[:, pl.ds(low - left, high - low)],
                    preferred_element_type=jnp.float32,
                ).astype(jnp.bfloat16)
            left += source.shape[1]

    def block(e):
        return pl.ds(pl.multiple_of(e * slots, 16), slots)

    def one_copy(i, p):
        size = pack_one.shape[1] // ONE_CUTS
        at = pl.ds(pl.multiple_of(p * size, 128), size)
        return remote(
            pack_one.at[block(peer(i)), at],
            rows_in.at[block(me), at],
            one_send.at[i, p],
            one_recv.at[i, p],
            (dp, peer(i)),
        )

    def two_copy(i, p):
        at = group_at(p)
        return remote(
            pack_two.at[block(peer(i)), at],
            feats.at[block(me), at],
            two_send.at[i, p],
            two_recv.at[i, p],
            (dp, peer(i)),
        )

    def head_copy(i):
        source = (master_ref, one_ref, two_ref)[i]
        return remote(
            source.at[0, :, pl.ds(0, heads_in.shape[2])],
            heads_in.at[i],
            head_send.at[i],
            head_recv.at[i],
            lower,
        )

    loads[0].wait()
    shard = down_in[...].astype(jnp.float32)
    if raw.shape[0] > share:
        spare = jnp.zeros((raw.shape[0] - share, depth), jnp.float32)
        shard = jnp.concatenate([shard, spare], axis=0)
    raw[...] = shard.astype(jnp.bfloat16)
    pl.semaphore_wait(barrier, experts + 4)
    for h in range(2):
        for d in range(2):
            raw_copy(d, h).start()
    first.start()
    pack_one[:, pl.ds(depth + 2 * hidden, 128)] = jnp.broadcast_to(
        slot_weight, (experts * slots, 128)
    ).astype(jnp.bfloat16)
    def joined(top, low):
        pieces = [top.astype(jnp.float32)[:share], low.astype(jnp.float32)[:share]]
        return jnp.concatenate(pieces, axis=0).astype(jnp.bfloat16)

    def share_first():
        first.wait()
        mine = raw[:, half_at(c)].astype(jnp.float32)
        theirs = raw_sib[...].astype(jnp.float32)
        down_all[c, place(z), :] = joined(
            jnp.where(c == 0, mine, theirs), jnp.where(c == 0, theirs, mine)
        )
        pass_copy(0, c).start()

    def forward(s):
        if s >= half:
            return
        if s == 1:
            for d in range(2):
                raw_land(d, 0).wait_recv()
                raw_land(d, 1).wait_recv()
                block_at = place(z - 1 if d == 0 else z + 1)
                down_all[c, block_at, :] = joined(raw_in[d, 0], raw_in[d, 1])
        for d, u in every:
            if s > 1:
                down_copy(d, u, s - 1).wait_recv()
            if d == u or s < half - 1:
                down_copy(d, u, s).start()
            if d == u and s == half - 1:
                twin_copy(d).start()
        pass_copy(n - s, c).start()
        pass_copy(s, c).start()

    loads[1].wait()
    loads[2].wait()
    for p in range(ONE_CUTS):
        pack(pack_one, ONE_CUTS, p, (grad_in, saved_in))
        if p == 0:
            share_first()
        for i in far:
            one_copy(i, p).start()
        forward(p + 1)
    loads[3].wait()
    for p in range(TWO_CUTS):
        pack_two[:, group_at(p)] = jnp.dot(
            select, tok_in[:, group_at(p)], preferred_element_type=jnp.float32
        ).astype(jnp.bfloat16)
        for i in far:
            two_copy(i, p).start()
        forward(p + ONE_CUTS + 1)
    for i in range(3):
        head_copy(i).start()
    rows_in[block(me), :] = pack_one[block(me), :]
    feats[block(me), :] = pack_two[block(me), :]

    for s in range(ONE_CUTS + TWO_CUTS + 1, half):
        forward(s)

    def land_one(i, _):
        for p in range(ONE_CUTS):
            one_copy(i, p).wait_recv()
        return 0

    lax.fori_loop(1, experts, land_one, 0)

    def land_pass(r, _):
        pass_copy(r, 1 - c).wait_recv()
        return 0

    lax.fori_loop(0, half - 1, land_pass, 0)
    lax.fori_loop(half + 2, n, land_pass, 0)
    for u in range(2):
        down_copy(u, u, half - 1).wait_recv()
        twin_copy(u).wait_recv()
    land_pass(half - 1, 0)
    land_pass(half + 1, 0)

    tile = 256
    weight = rows_in[:, pl.ds(depth + 2 * hidden, 128)].astype(jnp.float32)[:, :1]
    total = jnp.zeros((experts * slots, 1), jnp.float32)
    for j in range(hidden // tile):
        back = sum(
            lax.dot_general(
                rows_in[:, pl.ds(h * 2 * part, 2 * part)],
                down_all[h, pl.ds(j * tile, tile), :],
                (((1,), (1,)), ((), ())),
                preferred_element_type=jnp.float32,
            )
            for h in range(2)
        )
        gate = rows_in[:, pl.ds(depth + j * tile, tile)].astype(jnp.float32)
        up = rows_in[:, pl.ds(depth + hidden + j * tile, tile)].astype(jnp.float32)
        sig = 1.0 / (1.0 + jnp.exp(-gate))
        silu = gate * sig
        total = total + jnp.sum(silu * up * back, axis=1, keepdims=True)
        scaled = weight * back
        dgu[:, pl.ds(j * tile, tile)] = (
            scaled * up * sig * (1.0 + gate * (1.0 - sig))
        ).astype(jnp.bfloat16)
        dgu[:, pl.ds(hidden + j * tile, tile)] = (scaled * silu).astype(jnp.bfloat16)
    score[...] = jnp.broadcast_to(total, score.shape)

    def score_copy(i):
        return remote(
            score.at[pl.ds(pl.multiple_of(peer(i) * slots, 8), slots)],
            score_in.at[pl.ds(pl.multiple_of(me * slots, 8), slots)],
            score_send.at[i],
            score_recv.at[i],
            (dp, peer(i)),
        )

    def land_two(p):
        def land(i, _):
            two_copy(i, p).wait_recv()
            return 0

        lax.fori_loop(1, experts, land, 0)
        at = group_at(p)
        feat_t[at, :] = feats[:, at].T

    def sib_copy(r):
        return remote(give.at[r], sib.at[r], sib_send.at[r], sib_recv.at[r], other)

    def ring_copy(d, u, s):
        return [
            remote(
                buffer.at[d, u, s],
                buffer.at[d, u, s + 1],
                send.at[d, u, s],
                recv.at[d, u, s],
                (ahead, behind)[d],
            )
            for buffer, send, recv in (
                (work, sum_send, sum_recv),
                (scale, scale_send, scale_recv),
            )
        ]

    late, early = pl.ds(rows - 16, 16), pl.ds(0, rows - 16)

    def last_copy(d, u, pieces=(0, 1, 2)):
        s = half - 1
        parts = (
            (scale.at[d, u, s], scale.at[d, u, s + 1], scale_send, scale_recv),
            (work.at[d, u, s, late], work.at[d, u, s + 1, late], sum_send, sum_recv),
            (work.at[d, u, s, early], work.at[d, u, s + 1, early], rest_send, rest_recv),
        )
        copies = []
        for i in pieces:
            source, target, send, recv = parts[i]
            slot = (d, u) if i == 2 else (d, u, s)
            copies.append(
                remote(source, target, send.at[slot], recv.at[slot], (ahead, behind)[d])
            )
        return copies

    def produce(places):
        pieces = []
        for r in places:
            owner = lax.rem(z + r, n)
            for core in (c, 1 - c):
                start = pl.multiple_of((owner * 2 + core) * rows, 16)
                pieces.append(feat_t[pl.ds(start, rows), :])
        lhs = jnp.concatenate(pieces, axis=0)
        for j in range(width // 256):
            at = pl.ds(j * 256, 256)
            prod = jnp.dot(lhs, dgu[:, at], preferred_element_type=jnp.float32)
            prod = prod.astype(jnp.bfloat16)
            for i, r in enumerate(places):
                own[r, :, at] = prod[2 * i * rows : (2 * i + 1) * rows]
                give[r, :, at] = prod[(2 * i + 1) * rows : (2 * i + 2) * rows]

    def chip_sum(r, u, at=pl.ds(0, rows)):
        across = pl.ds(u * cols, cols)
        return own[r, at, across].astype(jnp.float32) + sib[r, at, across].astype(jnp.float32)

    def decoded(d, u, s, at=pl.ds(0, rows)):
        return work[d, u, s, at, :].astype(jnp.int32).astype(jnp.float32) * scale[d, u, s]

    def step(s, streams, fresh, last=False):
        k = half - s
        for d, u in streams:
            r = k if d == 0 else n - k
            value = chip_sum(r, u)
            if (d, u) not in fresh:
                for copy in ring_copy(d, u, s - 1):
                    copy.wait_recv()
                value = value + decoded(d, u, s)
            most = jnp.maximum(jnp.max(jnp.abs(value), axis=0, keepdims=True), 1e-30)
            scale[d, u, s] = most * (1.0 / 32767.0)
            coded = jnp.round(value * (32767.0 / most))
            work[d, u, s] = coded.astype(jnp.int32).astype(jnp.int16)
            for copy in last_copy(d, u) if last else ring_copy(d, u, s):
                copy.start()

    groups = [groups_needed(t, span) for t in range(half + 1)]
    needed = [min(t for t in range(half + 1) if groups[t] > p) for p in range(TWO_CUTS)]

    def prepare(t):
        for p in range(TWO_CUTS):
            if needed[p] == t:
                land_two(p)
        k = half - t
        places = [k] if k in (0, half) else [k, n - k]
        produce(places)
        for r in places:
            sib_copy(r).start()

    prepare(0)
    prepare(1)
    sib_copy(half).wait_recv()
    step(0, every[:2], every[:2])
    prepare(2)

    def send_score(i, _):
        score_copy(i).start()
        return 0

    lax.fori_loop(1, experts, send_score, 0)
    mine_at = pl.ds(pl.multiple_of(me * slots, 8), slots)
    score_in[mine_at, :] = score[mine_at, :]

    def drain_sum(s, _):
        for d, u in every:
            for copy in ring_copy(d, u, s):
                copy.wait_send()
        return 0

    def drain_one():
        def drain(i, _):
            for p in range(ONE_CUTS):
                one_copy(i, p).wait_send()
            return 0

        lax.fori_loop(1, experts, drain, 0)

    def drain_two():
        def drain(i, _):
            for p in range(TWO_CUTS):
                two_copy(i, p).wait_send()
            return 0

        lax.fori_loop(1, experts, drain, 0)

    def drain_gather():
        def drain_pass(r, _):
            pass_copy(r, c).wait_send()
            return 0

        lax.fori_loop(0, half, drain_pass, 0)
        lax.fori_loop(half + 1, n, drain_pass, 0)

        def drain_down(s, _):
            for d, u in every:
                down_copy(d, u, s).wait_send()
            return 0

        lax.fori_loop(1, half - 1, drain_down, 0)
        for d in range(2):
            for h in range(2):
                raw_copy(d, h).wait_send()
        for u in range(2):
            down_copy(u, u, half - 1).wait_send()
            twin_copy(u).wait_send()

    def land_score():
        def land(i, _):
            score_copy(i).wait()
            return 0

        lax.fori_loop(1, experts, land, 0)
        for i in range(3):
            head_copy(i).wait()

    chores = (drain_one, drain_two, drain_gather, land_score)

    def body(s, _):
        k = half - s
        sib_copy(k).wait_recv()
        sib_copy(n - k).wait_recv()

        @pl.when(s == 1)
        def _():
            step(s, every, every[2:])

        @pl.when(s > 1)
        def _():
            step(s, every, ())

        for p in range(TWO_CUTS):
            if needed[p] > 2:

                @pl.when(s + 2 == needed[p])
                def _():
                    land_two(p)

        produce([k - 2, n - k + 2])
        sib_copy(k - 2).start()
        sib_copy(n - k + 2).start()

        @pl.when(s > 1)
        def _():
            drain_sum(s - 1, 0)

        for i, chore in enumerate(chores):
            if i + 1 < half - 2:
                pl.when(s == i + 1)(chore)
        return 0

    lax.fori_loop(1, half - 2, body, 0)
    for i, chore in enumerate(chores):
        if i + 1 >= half - 2:
            chore()
    for s in range(max(1, half - 2), half):
        k = half - s
        sib_copy(k).wait_recv()
        sib_copy(n - k).wait_recv()
        step(s, every, every[2:] if s == 1 else (), s == half - 1)
        if k == 2:
            prepare(half)

    heads_ref[...] = heads_in[...]
    router_ref[...] = jnp.sum(chosen * score_in[...], axis=0, keepdims=True)

    for d, u in every[:2]:
        for copy in ring_copy(d, u, 0):
            copy.wait_send()
    for s in range(max(1, half - 3), half - 1):
        drain_sum(s, 0)
    sib_copy(0).wait_recv()

    def finish(at, pieces):
        for u in range(2):
            for d in range(2):
                for copy in last_copy(d, u, pieces):
                    copy.wait_recv()
            out_ref[at, pl.ds(u * cols, cols)] = chip_sum(0, u, at) + (
                decoded(0, u, half, at) + decoded(1, u, half, at)
            )

    finish(late, (0, 1))
    last = remote(out_ref.at[pl.ds(rows - 8, 8)], tail_in, tail_send, tail_recv, upper)
    last.start()
    finish(early, (2,))

    def drain_sib(r, _):
        sib_copy(r).wait_send()
        return 0

    lax.fori_loop(0, n, drain_sib, 0)
    for d, u in every:
        for copy in last_copy(d, u):
            copy.wait_send()
    last.wait()
    tail_ref[...] = tail_in[...]


def weight_gradient(
    tokens, out_grad, saved, weight, routes, down, states, margin, n, experts, slots
):
    count, depth = tokens.shape
    hidden = saved.shape[1] // 2
    width = 2 * hidden
    total = experts * slots
    rows = depth // (2 * n)
    half = n // 2
    wide = depth + width + 128
    padded = -(-down.shape[0] // 16) * 16
    dma = pltpu.SemaphoreType.DMA
    bf16, f32 = jnp.bfloat16, jnp.float32
    anywhere = pl.BlockSpec(memory_space=pl.ANY)
    inside = pl.BlockSpec(memory_space=pltpu.VMEM)
    return pl.pallas_call(
        functools.partial(grad_kernel, n, experts),
        out_shape=(
            jax.ShapeDtypeStruct((rows, width), f32),
            jax.ShapeDtypeStruct((8, width), f32),
            jax.ShapeDtypeStruct((1, count), f32),
            jax.ShapeDtypeStruct((3, 1, margin), f32),
        ),
        in_specs=[anywhere, anywhere, anywhere, inside, inside] + [anywhere] * 4,
        out_specs=[inside] * 4,
        scratch_shapes=[
            pltpu.VMEM(tokens.shape, bf16),
            pltpu.VMEM(out_grad.shape, bf16),
            pltpu.VMEM(saved.shape, bf16),
            pltpu.VMEM(down.shape, bf16),
            pltpu.VMEM((total, wide), bf16),
            pltpu.VMEM((total, depth), bf16),
            pltpu.VMEM((total, wide), bf16),
            pltpu.VMEM((total, depth), bf16),
            pltpu.VMEM((padded, depth), bf16),
            pltpu.VMEM((2, 2, padded, depth // 2), bf16),
            pltpu.VMEM((padded, depth // 2), bf16),
            pltpu.VMEM((2, hidden, depth // 2), bf16),
            pltpu.VMEM((total, width), bf16),
            pltpu.VMEM((total, count), f32),
            pltpu.VMEM((total, count), f32),
            pltpu.VMEM((depth, total), bf16),
            pltpu.VMEM((n, rows, width), bf16),
            pltpu.VMEM((n, rows, width), bf16),
            pltpu.VMEM((n, rows, width), bf16),
            pltpu.VMEM((2, 2, half + 1, rows, width // 2), jnp.int16),
            pltpu.VMEM((2, 2, half + 1, 1, width // 2), f32),
            pltpu.VMEM((8, width), f32),
            pltpu.VMEM((3, 1, margin), f32),
            dma((4,)),
            dma((experts, ONE_CUTS)),
            dma((experts, ONE_CUTS)),
            dma((experts, TWO_CUTS)),
            dma((experts, TWO_CUTS)),
            dma((2, 2, half)),
            dma((2, 2, half)),
            dma((n,)),
            dma((n,)),
            dma((2,)),
            dma((2,)),
            dma,
            dma,
            dma((2, 2)),
            dma((2, 2)),
            dma((experts,)),
            dma((experts,)),
            dma((n,)),
            dma((n,)),
            dma((2, 2, half)),
            dma((2, 2, half)),
            dma((2, 2, half)),
            dma((2, 2, half)),
            dma((2, 2)),
            dma((2, 2)),
            dma,
            dma,
            dma((3,)),
            dma((3,)),
        ],
        compiler_params=pltpu.CompilerParams(
            collective_id=0, has_side_effects=True, vmem_limit_bytes=60 * 2**20
        ),
        cost_estimate=pl.CostEstimate(
            flops=2 * total * (depth * hidden + depth * width + count * wide),
            bytes_accessed=2 * count * wide,
            transcendentals=total * hidden,
        ),
    )(
        tokens,
        out_grad,
        saved,
        weight.reshape(1, count),
        routes.reshape(1, count),
        down,
        *states,
    )


def shift_load(ref, offset, row, count):
    start, lead = offset // 128 + row, lax.rem(offset, 128)
    lane = lax.broadcasted_iota(jnp.int32, (count, 128), 1)
    turn = lax.rem(128 - lead, 128)
    this = pltpu.roll(ref[pl.ds(start, count), :], turn, 1)
    following = pltpu.roll(ref[pl.ds(start + 1, count), :], turn, 1)
    return jnp.where(lane < 128 - lead, this, following)


def adam(grad, master, moment_one, moment_two):
    moment_new = beta_one * moment_one + (1.0 - beta_one) * grad
    square_new = beta_two * moment_two + (1.0 - beta_two) * grad * grad
    update = (moment_new * (1.0 / (1.0 - beta_one**adam_step))) / (
        jnp.sqrt(square_new * (1.0 / (1.0 - beta_two**adam_step))) + adam_eps
    )
    return master - learn_rate * (update + decay_rate * master), moment_new, square_new


def step_kernel(
    offset_ref,
    block_ref,
    below_ref,
    heads_ref,
    master_ref,
    one_ref,
    two_ref,
    router_ref,
    new_master_ref,
    new_one_ref,
    new_two_ref,
    weight_ref,
    new_router_ref,
    ext,
    states,
    made,
    flat,
    head_made,
    block,
    below,
    heads,
    in_sem,
    out_sem,
):
    rows, width = block_ref.shape
    lines = width // 128
    even = rows * lines
    position = lax.axis_index("dp")
    lead = offset_ref[position] - position * (even * 128)
    tail = offset_ref[position + 1] - (position + 1) * (even * 128)
    slots = master_ref.shape[2] // 128
    extra = slots - even
    ahead = 8 * lines
    sources = (master_ref, one_ref, two_ref)
    results = (new_master_ref, new_one_ref, new_two_ref)
    pairs = [(block_ref, block), (below_ref, below), (router_ref, new_router_ref)]
    for i in range(3):
        pairs.append((sources[i].reshape(slots, 128), states.at[i]))
        pairs.append((heads_ref.at[i].reshape(heads.shape[1], 128), heads.at[i]))
    loads = [pltpu.make_async_copy(*pair, in_sem.at[i]) for i, pair in enumerate(pairs)]
    for load in loads:
        load.start()
    for load in loads[:2]:
        load.wait()
    for g in range(lines):
        at = pl.ds(g * 128, 128)
        ext[pl.ds(g, 8, lines), :] = below[:, at]
        ext[pl.ds(ahead + g, rows, lines), :] = block[:, at]
    after = ahead + even
    ext[pl.ds(after, ext.shape[0] - after), :] = jnp.zeros((ext.shape[0] - after, 128), jnp.float32)
    held = even * 128 + tail - lead
    for load in loads[2:]:
        load.wait()

    def run(row, count):
        index = (
            (row + lax.broadcasted_iota(jnp.int32, (count, 128), 0)) * 128
            + lax.broadcasted_iota(jnp.int32, (count, 128), 1)
        )
        inside = index < held
        grad = jnp.where(inside, shift_load(ext, ahead * 128 + lead, row, count), 0.0)
        at = pl.ds(row, count)
        fresh = adam(grad, states[0, at, :], states[1, at, :], states[2, at, :])
        for i in range(3):
            made[i, at, :] = jnp.where(inside, fresh[i], 0.0)

    def out(i, first, count):
        at = pl.ds(first, count)
        target = results[i].reshape(slots, 128).at[at]
        return pltpu.make_async_copy(made.at[i, at], target, out_sem.at[i, first // PART])

    parts = [(first, min(PART, slots - first)) for first in range(0, slots, PART)]
    for first, count in parts:
        whole = count // 32

        def some(k, _):
            run(pl.multiple_of(first + k * 32, 8), 32)
            return 0

        lax.fori_loop(0, whole, some, 0, unroll=True)
        if count % 32:
            run(first + whole * 32, count % 32)
        for i in range(3):
            out(i, first, count).start()

    head_rows = heads.shape[1]
    grad = shift_load(ext, (ahead + even) * 128 + tail, 0, head_rows)
    head_made[pl.ds(0, 32), :] = jnp.zeros((32, 128), jnp.float32)
    head_made[pl.ds(32, head_rows), :] = adam(grad, heads[0], heads[1], heads[2])[0]

    def lay(row, count):
        return shift_load(made.at[0], -lead, row, count)

    def some_rows(k, _):
        row = pl.multiple_of(k * 32, 8)
        flat[pl.ds(row, 32), :] = lay(row, 32)
        return 0

    lax.fori_loop(0, even // 32 - 1, some_rows, 0, unroll=True)
    index = lax.broadcasted_iota(jnp.int32, (32, 128), 0) * 128 + lax.broadcasted_iota(
        jnp.int32, (32, 128), 1
    )
    flat[pl.ds(even - 32, 32), :] = jnp.where(
        index < 32 * 128 + tail, lay(even - 32, 32), shift_load(head_made, -tail, 0, 32)
    )
    for g in range(lines):
        weight_ref[:, pl.ds(g * 128, 128)] = flat[pl.ds(g, rows, lines), :].astype(jnp.bfloat16)
    for first, count in parts:
        for i in range(3):
            out(i, first, count).wait()


PART = 256


def bucket_step(offsets, row_block, below, heads, master, moment_one, moment_two, router):
    rows, width = row_block.shape
    slots = master.shape[2] // 128
    f32 = jnp.float32
    inside = pl.BlockSpec(memory_space=pltpu.VMEM)
    anywhere = pl.BlockSpec(memory_space=pl.ANY)
    lines = width // 128
    total = -(-(9 + 8 * lines + slots + 32) // 8) * 8
    made_rows = -(-(slots + 10) // 8) * 8
    return pl.pallas_call(
        step_kernel,
        out_shape=[jax.ShapeDtypeStruct(master.shape, f32)] * 3
        + [
            jax.ShapeDtypeStruct((rows, width), jnp.bfloat16),
            jax.ShapeDtypeStruct(router.shape, f32),
        ],
        in_specs=[pl.BlockSpec(memory_space=pltpu.SMEM)] + [anywhere] * 7,
        out_specs=[anywhere] * 3 + [inside, anywhere],
        scratch_shapes=[
            pltpu.VMEM((total, 128), f32),
            pltpu.VMEM((3, slots, 128), f32),
            pltpu.VMEM((3, made_rows, 128), f32),
            pltpu.VMEM((rows * lines, 128), f32),
            pltpu.VMEM((72, 128), f32),
            pltpu.VMEM(row_block.shape, f32),
            pltpu.VMEM(below.shape, f32),
            pltpu.VMEM((3, heads.shape[2] // 128, 128), f32),
            pltpu.SemaphoreType.DMA((9,)),
            pltpu.SemaphoreType.DMA((3, -(-slots // PART))),
        ],
        compiler_params=pltpu.CompilerParams(vmem_limit_bytes=60 * 2**20),
    )(offsets, row_block, below, heads, master, moment_one, moment_two, router)


def shards(
    tokens,
    out_grad,
    gate_up,
    route_weight,
    routes,
    down_weight,
    master,
    moment_one,
    moment_two,
    offsets,
):
    token_count, model_width = tokens.shape
    choice_count = routes.shape[1]
    hidden = gate_up.shape[2] // 2
    local_experts = master.shape[0]
    bucket_cap = master.shape[2]
    groups = lax.axis_size("expert")
    dp_count = lax.axis_size("dp")
    experts = groups * local_experts
    n = dp_count // 2
    row_count = token_count * choice_count
    capacity = 2 * row_count // experts
    flat_size = model_width * 2 * hidden
    even_size = flat_size // dp_count
    margin_size = bucket_cap - even_size
    states = (master, moment_one, moment_two)
    row_block, below_rows, router_row, heads = weight_gradient(
        tokens,
        out_grad,
        gate_up.reshape(row_count, 2 * hidden),
        route_weight,
        routes,
        down_weight[0],
        states,
        margin_size,
        n,
        experts,
        capacity,
    )
    fresh = bucket_step(offsets, row_block, below_rows, heads, *states, router_row)
    return (
        *fresh[:3],
        fresh[3].reshape(1, model_width // dp_count, 2 * hidden),
        fresh[4].reshape(token_count, choice_count),
    )


def solution(mesh):
    placed = (
        P(("dp", "expert"), None),
        P(("dp", "expert"), None),
        P(("dp", "expert"), None, None),
        P(("dp", "expert"), None),
        P(("dp", "expert"), None),
        P("expert", "dp", None),
        P("expert", "dp", None),
        P("expert", "dp", None),
        P("expert", "dp", None),
        P(),
    )
    return jax.shard_map(
        shards,
        mesh=mesh,
        in_specs=placed,
        out_specs=(
            P("expert", "dp", None),
            P("expert", "dp", None),
            P("expert", "dp", None),
            P("expert", "dp", None),
            P(("dp", "expert"), None),
        ),
        check_vma=False,
    )
```
